1024 devices in a mesh: row: 8 (over x, core), col: 128 (over y, z).
Axes of the slice: x: 4, y: 4, z: 32, core: 2. Of those that a mesh axis runs over, the one named last changes fastest.
Arguments:
- fields: float32 [1024, 4, 32, 1024], P(('row', 'col')), may hold values from -6 to 6
- fluid_mask: int32 [1024, 32, 1024], P(('row', 'col')), may hold values 0 or 1
- body_force: float32 [3], replicated, may hold values from -3 to 3
- neighbours: int32 [1024, 6], P(('row', 'col')), may hold values from -1 to 0, as said below
- sources: int32 [1024, 8], P(('row', 'col')), may hold values from -1 to 127, as said below
Outputs:
- new_fields: float32 [1024, 4, 32, 1024], P(('row', 'col'))
- coarse_residual: float32 [1024, 512], P(('row', 'col'))
The draws below stay inside these ranges and needn't reach their ends.
Inputs may be any that keep to these rules, and one draw needn't show every extreme that they name: `neighbours`: entries 0 and 1 name a slot on the device one lower or higher along row, 2 and 3 along col, 4 and 5 on the own device; links are mutual. `sources`: every fine tile of a row group is named exactly once among that row group's entries; one device's entries name at most 4 tiles, and some device reaches that in every draw.
All inputs are finite; a program needn't handle non-finite values. No bound on the sum of `fluid_mask` on one device may be relied on, other than what follows from the above.
Results may differ from the reference program's by a relative error of at most 0.00002.
Values sent between devices are 32-bit elements; how exact they have to be, the bound alone decides.
A program may use at most 32 MiB of HBM per device.

```python
import jax
import jax.numpy as jnp
from jax import lax

TILES_DEV = 1
TILE = 32
SWEEPS = 2
ROW_GROUPS = 8
COL_GROUPS = 128
TILES_ALL = 1024
COARSE_DEV = 1
COARSE_ALL = 1024


def draw_neighbours(key, part):
    key = jax.random.fold_in(key, 11)
    order_key, link_key = jax.random.split(key)
    row_total = ROW_GROUPS
    col_total = COL_GROUPS
    depth_total = TILES_DEV
    scores = jax.random.randint(order_key, (row_total, col_total, depth_total), 0, 1 << 20) * depth_total + jnp.arange(depth_total, dtype=jnp.int32)
    slot_order = jnp.argsort(scores, axis=2).astype(jnp.int32)
    height = jnp.argsort(slot_order, axis=2).astype(jnp.int32)
    link_list = jax.random.randint(link_key, (3, row_total, col_total, depth_total), 0, 4) > 0
    minus_one = jnp.int32(-1)
    plus_x = jnp.where(link_list[0], jnp.roll(slot_order, -1, axis=0), minus_one).at[-1].set(-1)
    minus_x = jnp.where(jnp.roll(link_list[0], 1, axis=0), jnp.roll(slot_order, 1, axis=0), minus_one).at[0].set(-1)
    plus_y = jnp.where(link_list[1], jnp.roll(slot_order, -1, axis=1), minus_one).at[:, -1].set(-1)
    minus_y = jnp.where(jnp.roll(link_list[1], 1, axis=1), jnp.roll(slot_order, 1, axis=1), minus_one).at[:, 0].set(-1)
    plus_z = jnp.where(link_list[2], jnp.roll(slot_order, -1, axis=2), minus_one).at[:, :, -1].set(-1)
    minus_z = jnp.where(jnp.roll(link_list[2], 1, axis=2), jnp.roll(slot_order, 1, axis=2), minus_one).at[:, :, 0].set(-1)
    by_height = jnp.stack([minus_x, plus_x, minus_y, plus_y, minus_z, plus_z], axis=3)
    by_slot = jnp.take_along_axis(by_height, height[..., None], axis=2)
    return by_slot.reshape(row_total * col_total * depth_total, 6).astype(jnp.int32)


def draw_sources(key, part):
    key = jax.random.fold_in(key, 29)
    full_key, lead_key, wide_key, narrow_key, order_key = jax.random.split(key, 5)
    row_total = ROW_GROUPS
    block_total = COL_GROUPS // 4
    slot_count = 8 * COARSE_DEV
    item_count = 4 * TILES_DEV
    item_total = COL_GROUPS * TILES_DEV
    full_block = jax.random.randint(full_key, (row_total, block_total), 0, 4) == 0
    full_block = full_block.at[0, 0].set(True)
    lead_device = jax.random.randint(lead_key, (row_total, block_total), 0, 4)
    wide_scores = jax.random.randint(wide_key, (row_total, block_total, 4 * slot_count), 0, 1 << 20) * (4 * slot_count) + jnp.arange(4 * slot_count, dtype=jnp.int32)
    wide_perm = jnp.argsort(wide_scores, axis=2).astype(jnp.int32)[..., :item_count]
    narrow_scores = jax.random.randint(narrow_key, (row_total, block_total, slot_count), 0, 1 << 20) * slot_count + jnp.arange(slot_count, dtype=jnp.int32)
    narrow_perm = jnp.argsort(narrow_scores, axis=2).astype(jnp.int32)[..., :item_count]
    target = jnp.where(full_block[..., None], lead_device[..., None] * slot_count + narrow_perm, wide_perm).astype(jnp.int32)
    order_scores = jax.random.randint(order_key, (row_total, item_total), 0, 1 << 20) * item_total + jnp.arange(item_total, dtype=jnp.int32)
    row_order = jnp.argsort(order_scores, axis=1).astype(jnp.int32)
    source_id = row_order.reshape(row_total, block_total, item_count)
    row_ids = jnp.broadcast_to(jnp.arange(row_total, dtype=jnp.int32)[:, None, None], target.shape)
    block_ids = jnp.broadcast_to(jnp.arange(block_total, dtype=jnp.int32)[None, :, None], target.shape)
    source_table = jnp.full((row_total, block_total, 4 * slot_count), -1, jnp.int32)
    source_table = source_table.at[row_ids, block_ids, target].set(source_id)
    return source_table.reshape(row_total * block_total * 4 * COARSE_DEV, 8)


def with_ends(result, rng, low, top_value):
    dims = result.shape
    spot = [jax.random.randint(jax.random.fold_in(rng, axis), (), 0, dims[axis]) for axis in range(len(dims))]
    result = result.at[tuple(spot)].set(low)
    longest = dims.index(max(dims))
    spot[longest] = (spot[longest] + 1) % dims[longest]
    return result.at[tuple(spot)].set(top_value)


def levels(own_key, shape, cuts, least, high):
    def one(axis_at, blocks):
        draws = jax.random.uniform(jax.random.fold_in(jax.random.fold_in(own_key, 6), axis_at), (blocks,), jnp.float32, least / len(cuts), high / len(cuts))
        return jnp.repeat(jnp.exp(draws), shape[axis_at] // blocks).reshape((-1,) + (1,) * (len(shape) - axis_at - 1))

    loudness = one(*cuts[0])
    for cut in cuts[1:]:
        loudness = loudness * one(*cut)
    return loudness


def normal_values(own_key, shape, scale, limit, pieces=(), kind=jnp.bfloat16):
    result = jax.random.normal(own_key, shape, jnp.float32) * scale
    if len(pieces) > 0:
        result = levels(own_key, shape, pieces, -0.22, 0.18) * result
    return jnp.clip(result, min=-limit, max=limit).astype(kind)


def setup_inputs(seed: int = 0) -> dict:
    key_of = jax.random.split(jax.random.key(seed), 6)
    return {
        "fields": normal_values(key_of[0], (TILES_ALL, 4, TILE, TILE * TILE), 1.0, 6.0, ((0, 1024),), jnp.float32),
        "fluid_mask": with_ends((jax.random.randint(key_of[1], (TILES_ALL, TILE, TILE * TILE), 0, 4) < 3).astype(jnp.int32), jax.random.fold_in(key_of[1], 1), 0, 1),
        "body_force": normal_values(key_of[2], (3,), 1.0, 3.0, (), jnp.float32),
        "neighbours": draw_neighbours(jax.random.fold_in(key_of[5], 71), 0),
        "sources": draw_sources(jax.random.fold_in(key_of[5], 71), 0),
    }


RELAXATION = 0.8
PRESSURE_RATE = 0.5


def tile_faces(values, edge_cells):
    low_x = values[:, :, 0, :]
    high_x = values[:, :, -1, :]
    low_y = values[..., :edge_cells]
    high_y = values[..., -edge_cells:]
    low_z = values[..., ::edge_cells]
    high_z = values[..., edge_cells - 1::edge_cells]
    return low_x, high_x, low_y, high_y, low_z, high_z


def neighbour_values(values, planes, edge_cells):
    minus_x, plus_x, minus_y, plus_y, minus_z, plus_z = planes
    below_x = jnp.concatenate([minus_x[:, :, None, :], values[:, :, :-1, :]], axis=2)
    above_x = jnp.concatenate([values[:, :, 1:, :], plus_x[:, :, None, :]], axis=2)
    below_y = jnp.concatenate([minus_y, values[..., :-edge_cells]], axis=3)
    above_y = jnp.concatenate([values[..., edge_cells:], plus_y], axis=3)
    depth_index = jnp.arange(edge_cells * edge_cells, dtype=jnp.int32) % edge_cells
    zero_col = jnp.zeros(values.shape[:3] + (1,), values.dtype)
    below_z = jnp.where(depth_index == 0, jnp.repeat(minus_z, edge_cells, axis=3), jnp.concatenate([zero_col, values[..., :-1]], axis=3))
    above_z = jnp.where(depth_index == edge_cells - 1, jnp.repeat(plus_z, edge_cells, axis=3), jnp.concatenate([values[..., 1:], zero_col], axis=3))
    return below_x, above_x, below_y, above_y, below_z, above_z


def velocity_step(fields, planes, fluid, body_force, edge_cells):
    velocity = fields[:, :3]
    pressure = fields[:, 3:]
    below_x, above_x, below_y, above_y, below_z, above_z = neighbour_values(fields, planes, edge_cells)
    beside_all = (below_x + above_x) + (below_y + above_y) + (below_z + above_z)
    laplace = beside_all[:, :3] - 6.0 * velocity
    gradient = jnp.concatenate([pressure - below_x[:, 3:], pressure - below_y[:, 3:], pressure - below_z[:, 3:]], axis=1)
    momentum_residual = body_force[None, :, None, None] + laplace - gradient
    return velocity + (RELAXATION / 6.0) * fluid[:, None] * momentum_residual


def pressure_step(velocity, pressure, above, fluid, edge_cells):
    plus_x, plus_y, plus_z = above
    along_x = velocity[:, 0]
    along_y = velocity[:, 1]
    along_z = velocity[:, 2]
    next_x = jnp.concatenate([along_x[:, 1:, :], plus_x[:, None, :]], axis=1)
    next_y = jnp.concatenate([along_y[..., edge_cells:], plus_y], axis=2)
    depth_index = jnp.arange(edge_cells * edge_cells, dtype=jnp.int32) % edge_cells
    zero_col = jnp.zeros(along_z.shape[:2] + (1,), along_z.dtype)
    next_z = jnp.where(depth_index == edge_cells - 1, jnp.repeat(plus_z, edge_cells, axis=2), jnp.concatenate([along_z[..., 1:], zero_col], axis=2))
    residual = fluid * ((next_x - along_x) + (next_y - along_y) + (next_z - along_z))
    return pressure + PRESSURE_RATE * residual[:, None], residual


def restrict(residual, edge_cells):
    tile_count = residual.shape[0]
    block_edge = edge_cells // 4
    coarse_grid = residual.reshape(tile_count, 4, block_edge, 4, block_edge, 4, block_edge)
    return jnp.sum(coarse_grid, axis=(2, 4, 6)).reshape(tile_count, 64) / float(block_edge * block_edge)


def assemble(octants):
    coarse_count = octants.shape[0]
    coarse_grid = octants.reshape(coarse_count, 2, 2, 2, 4, 4, 4)
    return coarse_grid.transpose(0, 1, 4, 2, 5, 3, 6).reshape(coarse_count, 512)


def neighbour_index(neighbours):
    tile_ids = jnp.arange(TILES_ALL, dtype=jnp.int32)
    device = tile_ids // TILES_DEV
    offsets = (-COL_GROUPS, COL_GROUPS, -1, 1, 0, 0)
    link_list = []
    for direction in range(6):
        slot_ids = neighbours[:, direction]
        tile_index = (device + offsets[direction]) * TILES_DEV + slot_ids
        tile_index = jnp.clip(tile_index, 0, TILES_ALL - 1).astype(jnp.int32)
        link_list.append((tile_index, slot_ids >= 0))
    return link_list


def fetch_plane(face, link):
    tile_index, present = link
    taken = jnp.take(face, tile_index, axis=0)
    return jnp.where(present.reshape((-1,) + (1,) * (face.ndim - 1)), taken, jnp.zeros((), face.dtype))


def reference(fields, fluid_mask, body_force, neighbours, sources):
    link_list = neighbour_index(neighbours)
    fluid = fluid_mask.astype(jnp.float32)
    blocks = TILES_ALL // 32

    def to_blocks(array):
        return array.reshape((blocks, 32) + array.shape[1:])

    def from_blocks(array):
        return array.reshape((TILES_ALL,) + array.shape[2:])

    residual = None
    for sweep_index in range(SWEEPS):
        low_x, high_x, low_y, high_y, low_z, high_z = tile_faces(fields, TILE)
        planes = (fetch_plane(high_x, link_list[0]), fetch_plane(low_x, link_list[1]), fetch_plane(high_y, link_list[2]), fetch_plane(low_y, link_list[3]), fetch_plane(high_z, link_list[4]), fetch_plane(low_z, link_list[5]))
        packed = (to_blocks(fields),) + tuple(to_blocks(plane) for plane in planes) + (to_blocks(fluid),)
        velocity = from_blocks(lax.map(lambda group: velocity_step(group[0], group[1:7], group[7], body_force, TILE), packed))
        above = (fetch_plane(velocity[:, 0, 0, :], link_list[1]), fetch_plane(velocity[:, 1, :, :TILE], link_list[3]), fetch_plane(velocity[:, 2, :, ::TILE], link_list[5]))
        packed = (to_blocks(velocity), to_blocks(fields[:, 3:]), to_blocks(above[0]), to_blocks(above[1]), to_blocks(above[2]), to_blocks(fluid))
        pressure, residual = lax.map(lambda group: pressure_step(group[0], group[1], group[2:5], group[5], TILE), packed)
        fields = jnp.concatenate([velocity, from_blocks(pressure)], axis=1)
        residual = from_blocks(residual)
    restricted = restrict(residual, TILE)
    coarse_ids = jnp.arange(COARSE_ALL, dtype=jnp.int32)
    row_base = (coarse_ids // COARSE_DEV) // COL_GROUPS * (COL_GROUPS * TILES_DEV)
    source_id = jnp.clip(row_base[:, None] + sources, 0, TILES_ALL - 1).astype(jnp.int32)
    octants = jnp.take(restricted, source_id.reshape(-1), axis=0).reshape(COARSE_ALL, 8, 64)
    octants = jnp.where((sources >= 0)[:, :, None], octants, jnp.zeros((), octants.dtype))
    return fields, assemble(octants)
```

```python
import functools

import jax
import jax.numpy as jnp
from jax import lax
from jax.experimental import pallas as pl
from jax.experimental.pallas import tpu as pltpu
from jax.sharding import PartitionSpec as P

MESH = pl.DeviceIdType.MESH
TILE = 32
RATE = 0.8 / 6.0
PRESSURE_RATE = 0.5
OFF = 8
PLANES = 48
NEAR = 5
FAR = 11
SLOTS = 33


def roll(values, shift, axis):
    return pltpu.roll(values, shift % values.shape[axis], axis)


def kernel(
    rows, y_count, z_count,
    neighbour_ref, source_ref, force_ref, fields_ref, mask_ref, fields_out, coarse_out,
    ext, mask_raw, vel1, pres1, vel2, pres2, halo0, halo1, halo2, gate_x, gate_lo, gate_hi,
    send_lo, send_hi, recv_lo, recv_hi, table, row_buf,
    load_sem, store_sem, send_sem, recv_sem, gsend_sem, grecv_sem, know_sem,
):
    f32 = jnp.float32
    cols = y_count * z_count
    r = lax.axis_index("row")
    c = lax.axis_index("col")
    y, z = c // z_count, lax.rem(c, z_count)

    def tile_at(dr, dc):
        return (lax.rem(r + dr + rows, rows), lax.rem(c + dc + cols, cols))

    def along(dy, dz):
        return (r, lax.rem(y + dy, y_count) * z_count + lax.rem(z + dz + z_count, z_count))

    greeted = [tile_at(dr, dc) for dr in (-1, 0, 1) for dc in (-1, 0, 1) if (dr, dc) != (0, 0)]
    greeted += [along(0, -1), along(0, 1)] + [along(j, 0) for j in range(1, y_count)]
    barrier = pltpu.get_barrier_semaphore()
    for device in greeted:
        pl.semaphore_signal(barrier, inc=1, device_id=device, device_id_type=MESH)

    loads = []
    for s in range(8):
        lanes = pl.ds(128 * s, 128)
        loads.append(pltpu.make_async_copy(fields_ref.at[:, :, lanes], ext.at[pl.ds(0, 4), pl.ds(OFF, TILE), s], load_sem.at[s]))
        loads.append(pltpu.make_async_copy(mask_ref.at[:, lanes], mask_raw.at[:, s], load_sem.at[8 + s]))
    for copy in loads:
        copy.start()

    sub = lax.broadcasted_iota(jnp.int32, (8, 128), 0)
    lane = lax.broadcasted_iota(jnp.int32, (8, 128), 1)
    depth = lane % TILE
    lane_long = lax.broadcasted_iota(jnp.int32, (PLANES, 128), 1)
    zero = jnp.zeros((8, 128), f32)
    one = jnp.ones((8, 128), f32)

    def link(direction, exists):
        return jnp.where(jnp.logical_and(neighbour_ref[0, direction] == 0, exists), 1.0, 0.0).astype(f32)

    links = [link(0, r > 0), link(1, r < rows - 1), link(2, c > 0), link(3, c < cols - 1), link(4, True), link(5, True)]
    own = zero
    for d in range(6):
        own = jnp.where(sub == d, links[d], own)

    for x in (0, 1, 2, 30, 31):
        ext[5, OFF + x] = own

    def flag(tile, d):
        return jnp.broadcast_to(tile[d : d + 1, :], (8, 128))

    own_z_lo = jnp.where(depth == 0, flag(own, 4), one)
    own_z_hi = jnp.where(depth == TILE - 1, flag(own, 5), one)
    gate_x[...] = jnp.ones((PLANES, 8, 128), f32)
    gate_x[OFF] = flag(own, 0)
    gate_x[OFF + TILE] = flag(own, 1)
    gate_lo[pl.ds(OFF, TILE)] = jnp.broadcast_to(own_z_lo[None], (TILE, 8, 128))
    gate_hi[pl.ds(OFF, TILE)] = jnp.broadcast_to(own_z_hi[None], (TILE, 8, 128))

    for copy in loads:
        copy.wait()
    ext[4, pl.ds(OFF, TILE)] = mask_raw[...].astype(f32)

    lane_tile = lax.broadcasted_iota(jnp.int32, (TILE, 128), 1)
    flags_tile = jnp.concatenate([own] * 4, axis=0)
    top = [ext[f, pl.ds(OFF, TILE), 7, :] for f in range(5)]
    send_hi[0] = jnp.where(lane_tile >= 64, top[0], roll(top[1], 64, 1))
    send_hi[1] = jnp.where(lane_tile >= 64, top[2], roll(top[3], 64, 1))
    send_hi[2] = jnp.where(lane_tile >= 64, top[4], flags_tile)
    low = [ext[f, pl.ds(OFF, TILE), 0, :] for f in range(5)]
    send_lo[0] = jnp.where(lane_tile < 96, low[0], flags_tile)
    send_lo[1] = low[1]
    send_lo[2] = low[2]
    send_lo[3] = jnp.where(lane_tile < 64, low[3], roll(low[4], 64, 1))

    pl.semaphore_wait(barrier, len(greeted))

    whole, first, last = pl.ds(OFF, TILE), pl.ds(0, 8), pl.ds(24, 8)
    below, above = pl.ds(0, 8), pl.ds(OFF + TILE, 8)
    plan = [
        (send_hi, recv_lo, slice(None), whole, (0, 1)),
        (send_lo, recv_hi, slice(None), whole, (0, -1)),
        (send_hi, recv_lo, last, below, (1, 1)),
        (send_hi, recv_lo, first, above, (-1, 1)),
        (send_lo, recv_hi, last, below, (1, -1)),
        (send_lo, recv_hi, first, above, (-1, -1)),
    ]
    faces = []
    for k, (src, dst, src_rows, dst_rows, offset) in enumerate(plan):
        faces.append(pltpu.make_async_remote_copy(
            src_ref=src if k < 2 else src.at[:, src_rows], dst_ref=dst.at[:, dst_rows], send_sem=send_sem.at[k], recv_sem=recv_sem.at[k],
            device_id=tile_at(*offset), device_id_type=MESH))
    faces.append(pltpu.make_async_remote_copy(
        src_ref=ext.at[:, pl.ds(OFF + 30, 2)], dst_ref=ext.at[:, pl.ds(OFF - 2, 2)], send_sem=send_sem.at[6], recv_sem=recv_sem.at[6],
        device_id=tile_at(1, 0), device_id_type=MESH))
    faces.append(pltpu.make_async_remote_copy(
        src_ref=ext.at[:, pl.ds(OFF, 3)], dst_ref=ext.at[:, pl.ds(OFF + TILE, 3)], send_sem=send_sem.at[7], recv_sem=recv_sem.at[7],
        device_id=tile_at(-1, 0), device_id_type=MESH))
    for copy in faces:
        copy.start()

    def tell(step, reach):
        for device in (along(0, reach), along(0, -reach)):
            pl.semaphore_signal(know_sem.at[step], inc=1, device_id=device, device_id_type=MESH)

    def hear(step):
        pl.semaphore_wait(know_sem.at[step], 2)

    tell(0, 1)
    hear(0)
    tell(1, 2)

    for copy in faces:
        copy.wait()

    row_lo, row_hi = ext[5, OFF - 1], ext[5, OFF + TILE]

    def spread_lo(tile):
        return jnp.where(lane < 64, tile, roll(tile, 64, 1))

    def spread_hi(tile):
        half = jnp.where(lane >= 96, tile, roll(tile, 96, 1))
        return jnp.where(lane >= 64, half, roll(half, 64, 1))

    col_lo = [spread_lo(recv_lo[2, k : k + 8]) for k in (0, OFF, OFF + TILE)]
    col_hi = [spread_hi(recv_hi[0, k : k + 8]) for k in (0, OFF, OFF + TILE)]
    mid = [row_lo, own, row_hi]
    for k, x, n in ((0, OFF - 2, 2), (2, OFF + TILE, 3)):
        gate_lo[pl.ds(x, n)] = jnp.broadcast_to(jnp.where(depth == 0, flag(mid[k], 4), one)[None], (n, 8, 128))
        gate_hi[pl.ds(x, n)] = jnp.broadcast_to(jnp.where(depth == TILE - 1, flag(mid[k], 5), one)[None], (n, 8, 128))

    def by_region(tiles):
        return jnp.concatenate([tiles[0]] + [tiles[1]] * 4 + [tiles[2]], axis=0)

    def strip_gates(outer, is_own, crossing, d):
        z_lo, z_hi, cross = [], [], []
        for k in range(3):
            z_lo.append(jnp.where(depth == 0, jnp.where(is_own, flag(mid[k], 4), flag(outer[k], 4)), one))
            z_hi.append(jnp.where(depth == TILE - 1, jnp.where(is_own, flag(mid[k], 5), flag(outer[k], 5)), one))
            cross.append(jnp.where(crossing, flag(mid[k], d), one))
        x_lo = jnp.where(sub == 0, jnp.where(is_own, flag(own, 0), flag(outer[1], 0)), one)
        x_hi = jnp.where(sub == 0, jnp.where(is_own, flag(own, 1), flag(outer[1], 1)), one)
        x_gate = jnp.concatenate([one, x_lo, one, one, one, x_hi], axis=0)
        return x_gate, by_region(cross), by_region(z_lo), by_region(z_hi)

    lo_gates = strip_gates(col_lo, lane >= 64, lane // TILE == 2, 2)
    hi_gates = strip_gates(col_hi, lane < 32, lane // TILE == 1, 3)
    cross_lo = by_region([flag(tile, 2) for tile in mid])
    cross_hi = by_region([flag(tile, 3) for tile in mid])

    raw = [recv_lo[0], recv_lo[1], recv_lo[2]]
    outer = [roll(raw[0], 64, 1), raw[0], roll(raw[1], 64, 1), raw[1], roll(raw[2], 64, 1)]
    lo = [jnp.where(lane_long < 64, outer[f], roll(ext[f, :, 0, :], 64, 1)) for f in range(5)]
    raw = [recv_hi[k] for k in range(4)]
    outer = [roll(raw[0], 32, 1), roll(raw[1], 32, 1), roll(raw[2], 32, 1), roll(raw[3], 32, 1), roll(raw[3], 96, 1)]
    hi = [jnp.where(lane_long < 32, roll(ext[f, :, 7, :], 32, 1), outer[f]) for f in range(5)]

    depth_long = lane_long % TILE

    def strip_below(v, gates):
        x_gate, y_gate, z_lo, _ = gates
        return (
            roll(v, 1, 0) * x_gate,
            roll(v, 32, 1) * y_gate,
            jnp.where(depth_long == 0, roll(v, -31, 1), roll(v, 1, 1)) * z_lo,
        )

    def strip_above(v, gates):
        x_gate, y_gate, _, z_hi = gates
        return (
            roll(v * x_gate, -1, 0),
            roll(v * y_gate, -32, 1),
            jnp.where(depth_long == TILE - 1, roll(v, 31, 1), roll(v, -1, 1)) * z_hi,
        )

    def strip_velocity(v, p, m, gates, wanted):
        under = strip_below(p, gates)
        result = []
        for d in wanted:
            b, a = strip_below(v[d], gates), strip_above(v[d], gates)
            laplace = (b[0] + a[0]) + (b[1] + a[1]) + (b[2] + a[2]) - 6.0 * v[d]
            result.append(v[d] + RATE * m * (force_ref[d] + laplace - (p - under[d])))
        return result

    def strip_pressure(v, p, m, gates):
        total = zero_strip
        for d in range(3):
            total = total + (strip_above(v[d], gates)[d] - v[d])
        return p + PRESSURE_RATE * (m * total)

    zero_strip = jnp.zeros((PLANES, 128), f32)

    def put_lo(dst, v):
        dst[:, 0, :] = roll(v, 64, 1) * cross_lo

    def put_hi(dst, v):
        dst[:, 7, :] = roll(v, 96, 1) * cross_hi

    for f in range(4):
        put_lo(halo0.at[f], lo[f])
        if f < 3:
            put_hi(halo0.at[f], hi[f])
    lo1 = strip_velocity(lo[:3], lo[3], lo[4], lo_gates, (0, 1, 2))
    hi1 = strip_velocity(hi[:3], hi[3], hi[4], hi_gates, (0, 1, 2))
    for d in range(3):
        put_lo(halo1.at[d], lo1[d])
        put_hi(halo1.at[d], hi1[d])
    lo_p1 = strip_pressure(lo1, lo[3], lo[4], lo_gates)
    hi_p1 = strip_pressure(hi1, hi[3], hi[4], hi_gates)
    put_lo(halo1.at[3], lo_p1)

    def below_y(v, h):
        w = jnp.where(sub3 == 0, h, roll(v, 1, 1))
        return roll(jnp.where(lane3 >= 96, w, v), 32, 2)

    def above_y(v, h):
        w = jnp.where(sub3 == 7, h, roll(v, -1, 1))
        return roll(jnp.where(lane3 < 32, w, v), -32, 2)

    def below_z(v, g):
        return jnp.where(lane3 % TILE == 0, roll(v, -31, 2), roll(v, 1, 2)) * g

    def above_z(v, g):
        return jnp.where(lane3 % TILE == TILE - 1, roll(v, 31, 2), roll(v, -1, 2)) * g

    def planes(x, n):
        return pl.ds(OFF + x, n)

    def velocity_planes(x, n, v_in, p_in, halo, v_out):
        here, under, over = planes(x, n), planes(x - 1, n), planes(x + 1, n)
        g_under, g_over, g_lo, g_hi = gate_x[here], gate_x[over], gate_lo[here], gate_hi[here]
        scale = RATE * ext[4, here]
        p = p_in[here]
        p_below = (p_in[under] * g_under, below_y(p, halo[3, here]), below_z(p, g_lo))
        for d in range(3):
            v, h = v_in[d, here], halo[d, here]
            total = (v_in[d, under] * g_under + v_in[d, over] * g_over) + (below_y(v, h) + above_y(v, h))
            total = total + (below_z(v, g_lo) + above_z(v, g_hi)) - 6.0 * v
            v_out[d, here] = v + scale * (force_ref[d] + total - (p - p_below[d]))

    def divergence_planes(x, n, v_in, halo_y):
        here, over = planes(x, n), planes(x + 1, n)
        vx, vy, vz = v_in[0, here], v_in[1, here], v_in[2, here]
        total = (v_in[0, over] * gate_x[over] - vx) + (above_y(vy, halo_y[here]) - vy) + (above_z(vz, gate_hi[here]) - vz)
        return ext[4, here] * total

    step = 5
    shape3 = (step, 8, 128)
    sub3 = lax.broadcasted_iota(jnp.int32, shape3, 1)
    lane3 = lax.broadcasted_iota(jnp.int32, shape3, 2)
    for x in range(-1, 34, step):
        velocity_planes(x, step, ext, ext.at[3], halo0, vel1)

    hear(1)
    tell(2, 4)
    tell(3, 1)

    for x in range(-1, 32, step):
        pres1[planes(x, step)] = ext[3, planes(x, step)] + PRESSURE_RATE * divergence_planes(x, step, vel1, halo1.at[1])

    hi1 = [jnp.where(lane_long < 32, roll(vel1[d, :, 7, :], 32, 1), hi1[d]) for d in range(3)]
    hi_p1 = jnp.where(lane_long < 32, roll(pres1[:, 7, :], 32, 1), hi_p1)
    put_hi(halo2, strip_velocity(hi1, hi_p1, hi[4], hi_gates, (1,))[0])

    step = 3
    shape3 = (step, 8, 128)
    sub3 = lax.broadcasted_iota(jnp.int32, shape3, 1)
    lane3 = lax.broadcasted_iota(jnp.int32, shape3, 2)
    for x in range(0, 33, step):
        velocity_planes(x, step, vel1, pres1, halo1, vel2)

    step = 8
    shape3 = (step, 8, 128)
    sub3 = lax.broadcasted_iota(jnp.int32, shape3, 1)
    lane3 = lax.broadcasted_iota(jnp.int32, shape3, 2)
    message = zero
    for x in range(0, TILE, step):
        div = divergence_planes(x, step, vel2, halo2)
        pres2[pl.ds(x, step)] = pres1[planes(x, step)] + PRESSURE_RATE * div
        part = jnp.sum(div, axis=0)
        for shift in (1, 2, 4):
            part = part + jnp.where((lane // shift) % 2 == 0, roll(part, -shift, 1), roll(part, shift, 1))
        part = part + roll(part, 32, 1)
        part = part + roll(part, 64, 1)
        part = part + jnp.where(sub % 2 == 0, roll(part, -1, 0), roll(part, 1, 0))
        message = jnp.where(jnp.logical_and(lane // 32 == x // 8, sub == 2 * ((lane % 8) // 2)), part, message)
    table[0, z_count // 2] = jnp.sum(message, axis=0, keepdims=True) * (1.0 / 64.0)

    hear(3)
    middle = z_count // 2
    near = []
    for k in range(1, NEAR + 1):
        for sign in (1, -1):
            index = len(near)
            near.append(pltpu.make_async_remote_copy(
                src_ref=table.at[0, middle], dst_ref=table.at[0, middle - sign * k], send_sem=gsend_sem.at[index], recv_sem=grecv_sem.at[index],
                device_id=along(0, sign * k), device_id_type=MESH))
    for copy in reversed(near):
        copy.start()

    stores = []
    for s in range(8):
        lanes = pl.ds(128 * s, 128)
        stores.append(pltpu.make_async_copy(vel2.at[:, pl.ds(OFF, TILE), s], fields_out.at[pl.ds(0, 3), :, lanes], store_sem.at[s]))
        stores.append(pltpu.make_async_copy(pres2.at[:, s], fields_out.at[3, :, lanes], store_sem.at[8 + s]))
    for copy in stores:
        copy.start()

    hear(2)
    tell(4, 3)

    for copy in near:
        copy.wait()
    hear(4)
    block = pl.ds(middle - NEAR, 2 * NEAR + 1)
    far = []
    for k, sign in enumerate((1, -1)):
        landed = pl.ds(middle - NEAR - sign * FAR, 2 * NEAR + 1)
        index = len(near) + k
        far.append(pltpu.make_async_remote_copy(
            src_ref=table.at[0, block], dst_ref=table.at[0, landed], send_sem=gsend_sem.at[index], recv_sem=grecv_sem.at[index],
            device_id=along(0, sign * FAR), device_id_type=MESH))
    for copy in far:
        copy.start()
    for copy in far:
        copy.wait()
    across = []
    for j in range(1, y_count):
        index = len(near) + len(far) + j - 1
        across.append(pltpu.make_async_remote_copy(
            src_ref=table.at[0], dst_ref=table.at[y_count - j], send_sem=gsend_sem.at[index], recv_sem=grecv_sem.at[index],
            device_id=along(j, 0), device_id_type=MESH))
    for copy in across:
        copy.start()

    spot = lax.broadcasted_iota(jnp.int32, (128, 512), 1)
    entry = (spot // 64) % 4 * 32 + spot % 4 * 8 + (spot // 8) % 4 * 2
    pick = jnp.where(lax.broadcasted_iota(jnp.int32, (128, 512), 0) == entry, 1.0, 0.0).astype(f32)
    spot = lax.broadcasted_iota(jnp.int32, (8, 512), 1)
    octant = spot // 256 * 4 + (spot // 32) % 2 * 2 + (spot // 4) % 2
    holds = lax.broadcasted_iota(jnp.int32, (8, 512), 0) == octant

    for copy in across:
        copy.wait()
    for o in range(8):
        source = source_ref[0, o]
        kept = jnp.maximum(source, 0)
        dy = lax.rem(kept // z_count - y + y_count, y_count)
        dz = lax.rem(lax.rem(kept, z_count) - z + z_count + middle, z_count)
        taken = table[dy, dz]
        row_buf[pl.ds(o, 1), :] = jnp.where(source >= 0, taken, jnp.zeros_like(taken))
    spread = jnp.dot(row_buf[...], pick, preferred_element_type=f32, precision=lax.Precision.HIGHEST)
    coarse_out[...] = jnp.sum(jnp.where(holds, spread, 0.0), axis=0, keepdims=True)

    for copy in stores:
        copy.wait()


def on_device(rows, fields, fluid_mask, body_force, neighbours, sources):
    y_count, z_count = 4, 32
    f32 = jnp.float32
    volume = lambda n: pltpu.VMEM((n, PLANES, 8, 128), f32)
    planes = lambda: pltpu.VMEM((PLANES, 8, 128), f32)
    near = 2 * NEAR + 2 + y_count - 1
    any_space = pl.BlockSpec(memory_space=pl.ANY)
    scalars = pl.BlockSpec(memory_space=pltpu.SMEM)
    new_fields, coarse = pl.pallas_call(
        functools.partial(kernel, rows, y_count, z_count),
        out_shape=(
            jax.ShapeDtypeStruct((4, TILE, TILE * TILE), f32),
            jax.ShapeDtypeStruct((1, 512), f32),
        ),
        in_specs=[scalars, scalars, scalars, any_space, any_space],
        out_specs=(any_space, pl.BlockSpec(memory_space=pltpu.VMEM)),
        scratch_shapes=[
            volume(6),
            pltpu.VMEM((TILE, 8, 128), jnp.int32),
            volume(3),
            planes(),
            volume(3),
            pltpu.VMEM((TILE, 8, 128), f32),
            volume(4),
            volume(4),
            planes(),
            planes(),
            planes(),
            planes(),
            pltpu.VMEM((4, TILE, 128), f32),
            pltpu.VMEM((3, TILE, 128), f32),
            pltpu.VMEM((3, PLANES, 128), f32),
            pltpu.VMEM((4, PLANES, 128), f32),
            pltpu.VMEM((y_count, SLOTS, 1, 128), f32),
            pltpu.VMEM((8, 128), f32),
            pltpu.SemaphoreType.DMA((16,)),
            pltpu.SemaphoreType.DMA((16,)),
            pltpu.SemaphoreType.DMA((8,)),
            pltpu.SemaphoreType.DMA((8,)),
            pltpu.SemaphoreType.DMA((near,)),
            pltpu.SemaphoreType.DMA((near,)),
            pltpu.SemaphoreType.REGULAR((5,)),
        ],
        compiler_params=pltpu.CompilerParams(
            collective_id=0, has_side_effects=True, vmem_limit_bytes=60 * 1024 * 1024
        ),
    )(
        neighbours,
        sources,
        body_force,
        fields.reshape(4, TILE, TILE * TILE),
        fluid_mask.reshape(TILE, TILE * TILE),
    )
    return new_fields[None], coarse


def solution(mesh):
    return jax.shard_map(
        functools.partial(on_device, mesh.shape["row"]),
        mesh=mesh,
        in_specs=(
            P(("row", "col"), None, None, None),
            P(("row", "col"), None, None),
            P(),
            P(("row", "col"), None),
            P(("row", "col"), None),
        ),
        out_specs=(P(("row", "col"), None, None, None), P(("row", "col"), None)),
        check_vma=False,
    )
```

```python
import functools

import jax
import jax.numpy as jnp
from jax import lax
from jax.experimental import pallas as pl
from jax.experimental.pallas import tpu as pltpu
from jax.sharding import PartitionSpec as P

MESH = pl.DeviceIdType.MESH
TILE = 32
RATE = 0.8 / 6.0
PRESSURE_RATE = 0.5
OFF = 8
PLANES = 48
NEAR = 5
FAR = 11
SLOTS = 33
GATHER_COPIES = 2 * NEAR + 2 + 9


def roll(values, shift, axis):
    return pltpu.roll(values, shift % values.shape[axis], axis)


def kernel(
    rows, y_count, z_count,
    neighbour_hbm, source_hbm, force_hbm, fields_ref, mask_ref, fields_out, coarse_out,
    neighbour_ref, source_ref, force_ref,
    ext, mask_raw, vel1, pres1, vel2, pres2, halo1, halo2, gate_x, gate_lo, gate_hi,
    send_lo, send_hi, recv_lo, recv_hi, send_corner, recv_corner, table, row_buf,
    load_sem, store_sem, send_sem, recv_sem, gsend_sem, grecv_sem, know_sem,
):
    f32 = jnp.float32
    cols = y_count * z_count
    r = lax.axis_index("row")
    c = lax.axis_index("col")
    y, z = c // z_count, lax.rem(c, z_count)

    def tile_at(dr, dc):
        return (lax.rem(r + dr + rows, rows), lax.rem(c + dc + cols, cols))

    def along(dy, dz):
        return (r, lax.rem(y + dy, y_count) * z_count + lax.rem(z + dz + z_count, z_count))

    greeted = [tile_at(dr, dc) for dr in (-1, 1) for dc in (-1, 1)]
    greeted += [tile_at(0, -1), tile_at(0, 1), tile_at(-1, 0), tile_at(1, 0)]
    greeted += [along(0, -1), along(0, 1), along(1, 0), along(y_count - 1, 0)]
    barrier = pltpu.get_barrier_semaphore()
    for device in greeted:
        pl.semaphore_signal(barrier, inc=1, device_id=device, device_id_type=MESH)

    smalls = [
        pltpu.make_async_copy(neighbour_hbm, neighbour_ref, load_sem.at[16]),
        pltpu.make_async_copy(source_hbm, source_ref, load_sem.at[17]),
        pltpu.make_async_copy(force_hbm, force_ref, load_sem.at[18]),
    ]
    for copy in smalls:
        copy.start()

    loads = []
    for s in range(8):
        lanes = pl.ds(128 * s, 128)
        loads.append(pltpu.make_async_copy(fields_ref.at[:, :, lanes], ext.at[pl.ds(0, 4), pl.ds(OFF, TILE), s], load_sem.at[s]))
        loads.append(pltpu.make_async_copy(mask_ref.at[:, lanes], mask_raw.at[:, s], load_sem.at[8 + s]))
    for copy in loads:
        copy.start()

    sub = lax.broadcasted_iota(jnp.int32, (8, 128), 0)
    lane = lax.broadcasted_iota(jnp.int32, (8, 128), 1)
    depth = lane % TILE
    lane_long = lax.broadcasted_iota(jnp.int32, (PLANES, 128), 1)
    zero = jnp.zeros((8, 128), f32)
    one = jnp.ones((8, 128), f32)

    for copy in smalls:
        copy.wait()

    def link(direction, exists):
        return jnp.where(jnp.logical_and(neighbour_ref[0, direction] == 0, exists), 1.0, 0.0).astype(f32)

    links = [link(0, r > 0), link(1, r < rows - 1), link(2, c > 0), link(3, c < cols - 1), link(4, True), link(5, True)]
    own = zero
    for d in range(6):
        own = jnp.where(sub == d, links[d], own)

    for x in (0, 1, 2, 30, 31):
        ext[5, OFF + x] = own

    def flag(tile, d):
        return jnp.broadcast_to(tile[d : d + 1, :], (8, 128))

    own_z_lo = jnp.where(depth == 0, flag(own, 4), one)
    own_z_hi = jnp.where(depth == TILE - 1, flag(own, 5), one)
    gate_x[...] = jnp.ones((PLANES, 8, 128), f32)
    gate_x[OFF] = flag(own, 0)
    gate_x[OFF + TILE] = flag(own, 1)
    gate_lo[pl.ds(OFF, TILE)] = jnp.broadcast_to(own_z_lo[None], (TILE, 8, 128))
    gate_hi[pl.ds(OFF, TILE)] = jnp.broadcast_to(own_z_hi[None], (TILE, 8, 128))

    for copy in loads:
        copy.wait()
    ext[4, pl.ds(OFF, TILE)] = mask_raw[...].astype(f32)

    lane_tile = lax.broadcasted_iota(jnp.int32, (TILE, 128), 1)
    flags_tile = jnp.concatenate([own] * 4, axis=0)
    top = [ext[f, pl.ds(OFF, TILE), 7, :] for f in range(5)]
    send_hi[0] = jnp.where(lane_tile >= 64, top[0], roll(top[1], 64, 1))
    send_hi[1] = jnp.where(lane_tile >= 64, top[2], roll(top[3], 64, 1))
    send_hi[2] = jnp.where(lane_tile >= 64, top[4], flags_tile)
    low = [ext[f, pl.ds(OFF, TILE), 0, :] for f in range(5)]
    send_lo[0] = jnp.where(lane_tile < 64, low[0], roll(low[2], 64, 1))
    send_lo[1] = jnp.where(lane_tile < 96, low[1], flags_tile)
    send_lo[2] = jnp.where(lane_tile < 64, low[3], roll(low[4], 64, 1))

    def corner(packed, x, up):
        tile = jnp.where(sub == 6, flag(own, 4), flag(own, 5))
        for g in range(3):
            tile = jnp.where(sub // 2 == g, roll(packed[g, x : x + 8], 2 * g - up, 0), tile)
        return tile

    send_corner[0] = corner(send_hi, 24, 6)
    send_corner[1] = corner(send_hi, 0, 0)
    send_corner[2] = corner(send_lo, 24, 6)
    send_corner[3] = corner(send_lo, 0, 0)

    pl.semaphore_wait(barrier, len(greeted))

    plan = [(send_corner.at[k], recv_corner.at[k], offset) for k, offset in enumerate([(1, 1), (-1, 1), (1, -1), (-1, -1)])]
    plan += [(send_hi, recv_lo, (0, 1)), (send_lo, recv_hi, (0, -1))]
    faces = []
    for k, (src, dst, offset) in enumerate(plan):
        faces.append(pltpu.make_async_remote_copy(
            src_ref=src, dst_ref=dst, send_sem=send_sem.at[k], recv_sem=recv_sem.at[k], device_id=tile_at(*offset), device_id_type=MESH))
    faces.append(pltpu.make_async_remote_copy(
        src_ref=ext.at[:, pl.ds(OFF + 30, 2)], dst_ref=ext.at[:, pl.ds(OFF - 2, 2)], send_sem=send_sem.at[6], recv_sem=recv_sem.at[6],
        device_id=tile_at(1, 0), device_id_type=MESH))
    faces.append(pltpu.make_async_remote_copy(
        src_ref=ext.at[:, pl.ds(OFF, 3)], dst_ref=ext.at[:, pl.ds(OFF + TILE, 3)], send_sem=send_sem.at[7], recv_sem=recv_sem.at[7],
        device_id=tile_at(-1, 0), device_id_type=MESH))
    for copy in faces:
        copy.start()

    def tell(step, reach):
        for device in (along(0, reach), along(0, -reach)):
            pl.semaphore_signal(know_sem.at[step], inc=1, device_id=device, device_id_type=MESH)

    def hear(step):
        pl.semaphore_wait(know_sem.at[step], 2)

    tell(0, 1)
    for j in (1, y_count - 1):
        pl.semaphore_signal(know_sem.at[5], inc=1, device_id=along(j, 0), device_id_type=MESH)

    def iotas(shape):
        return lax.broadcasted_iota(jnp.int32, shape, 1), lax.broadcasted_iota(jnp.int32, shape, 2)

    def below_y(v, h):
        w = jnp.where(sub3 == 0, 0.0 if h is None else h, roll(v, 1, 1))
        return roll(jnp.where(lane3 >= 96, w, v), 32, 2)

    def above_y(v, h):
        w = jnp.where(sub3 == 7, 0.0 if h is None else h, roll(v, -1, 1))
        return roll(jnp.where(lane3 < 32, w, v), -32, 2)

    def below_z(v, g):
        return jnp.where(lane3 % TILE == 0, roll(v, -31, 2), roll(v, 1, 2)) * g

    def above_z(v, g):
        return jnp.where(lane3 % TILE == TILE - 1, roll(v, 31, 2), roll(v, -1, 2)) * g

    def planes(x, n):
        return pl.ds(OFF + x, n)

    def velocity_planes(x, n, v_in, p_in, halo, v_out):
        here, under, over = planes(x, n), planes(x - 1, n), planes(x + 1, n)
        g_under, g_over, g_lo, g_hi = gate_x[here], gate_x[over], gate_lo[here], gate_hi[here]
        scale = RATE * ext[4, here]
        p = p_in[here]
        p_below = (p_in[under] * g_under, below_y(p, None if halo is None else halo[3, here]), below_z(p, g_lo))
        for d in range(3):
            v, h = v_in[d, here], None if halo is None else halo[d, here]
            total = (v_in[d, under] * g_under + v_in[d, over] * g_over) + (below_y(v, h) + above_y(v, h))
            total = total + (below_z(v, g_lo) + above_z(v, g_hi)) - 6.0 * v
            v_out[d, here] = v + scale * (force_ref[d] + total - (p - p_below[d]))

    def divergence_planes(x, n, v_in, halo_y):
        here, over = planes(x, n), planes(x + 1, n)
        vx, vy, vz = v_in[0, here], v_in[1, here], v_in[2, here]
        total = (v_in[0, over] * gate_x[over] - vx) + (above_y(vy, halo_y[here]) - vy) + (above_z(vz, gate_hi[here]) - vz)
        return ext[4, here] * total

    step, shape3 = 5, (5, 8, 128)
    sub3, lane3 = iotas(shape3)
    for x in range(1, 31, step):
        velocity_planes(x, step, ext, ext.at[3], None, vel1)
        if x == 1:
            hear(0)
            tell(1, 2)

    for copy in faces:
        copy.wait()

    row_lo, row_hi = ext[5, OFF - 1], ext[5, OFF + TILE]

    def spread_lo(tile):
        return jnp.where(lane < 64, tile, roll(tile, 64, 1))

    def spread_hi(tile):
        half = jnp.where(lane >= 96, tile, roll(tile, 96, 1))
        return jnp.where(lane >= 64, half, roll(half, 64, 1))

    corners = [recv_corner[k] for k in range(4)]
    col_lo, col_hi = spread_lo(recv_lo[2, 0:8]), spread_hi(recv_hi[1, 0:8])
    z_lo_outer = [(flag(corners[k], 6), flag(col, 4), flag(corners[k + 1], 6)) for k, col in ((0, col_lo), (2, col_hi))]
    z_hi_outer = [(flag(corners[k], 7), flag(col, 5), flag(corners[k + 1], 7)) for k, col in ((0, col_lo), (2, col_hi))]
    mid = [row_lo, own, row_hi]
    for k, x, n in ((0, OFF - 2, 2), (2, OFF + TILE, 3)):
        gate_lo[pl.ds(x, n)] = jnp.broadcast_to(jnp.where(depth == 0, flag(mid[k], 4), one)[None], (n, 8, 128))
        gate_hi[pl.ds(x, n)] = jnp.broadcast_to(jnp.where(depth == TILE - 1, flag(mid[k], 5), one)[None], (n, 8, 128))

    def by_region(tiles):
        return jnp.concatenate([tiles[0]] + [tiles[1]] * 4 + [tiles[2]], axis=0)

    def strip_gates(side, col, is_own, crossing, d):
        z_lo, z_hi, cross = [], [], []
        for k in range(3):
            z_lo.append(jnp.where(depth == 0, jnp.where(is_own, flag(mid[k], 4), z_lo_outer[side][k]), one))
            z_hi.append(jnp.where(depth == TILE - 1, jnp.where(is_own, flag(mid[k], 5), z_hi_outer[side][k]), one))
            cross.append(jnp.where(crossing, flag(mid[k], d), one))
        x_lo = jnp.where(sub == 0, jnp.where(is_own, flag(own, 0), flag(col, 0)), one)
        x_hi = jnp.where(sub == 0, jnp.where(is_own, flag(own, 1), flag(col, 1)), one)
        x_gate = jnp.concatenate([one, x_lo, one, one, one, x_hi], axis=0)
        return x_gate, by_region(cross), by_region(z_lo), by_region(z_hi)

    lo_gates = strip_gates(0, col_lo, lane >= 64, lane // TILE == 2, 2)
    hi_gates = strip_gates(1, col_hi, lane < 32, lane // TILE == 1, 3)
    cross_lo = by_region([flag(tile, 2) for tile in mid])
    cross_hi = by_region([flag(tile, 3) for tile in mid])

    def strip(received, tiles, g):
        return jnp.concatenate([roll(tiles[0], 6 - 2 * g, 0), received[g], roll(tiles[1], -2 * g, 0)], axis=0)

    raw = [strip(recv_lo, corners[:2], g) for g in range(3)]
    outer = [roll(raw[0], 64, 1), raw[0], roll(raw[1], 64, 1), raw[1], roll(raw[2], 64, 1)]
    lo = [jnp.where(lane_long < 64, outer[f], roll(ext[f, :, 0, :], 64, 1)) for f in range(5)]
    raw = [strip(recv_hi, corners[2:], g) for g in range(3)]
    outer = [roll(raw[0], 32, 1), roll(raw[1], 32, 1), roll(raw[0], 96, 1), roll(raw[2], 32, 1), roll(raw[2], 96, 1)]
    hi = [jnp.where(lane_long < 32, roll(ext[f, :, 7, :], 32, 1), outer[f]) for f in range(5)]

    depth_long = lane_long % TILE

    def strip_below(v, gates):
        x_gate, y_gate, z_lo, _ = gates
        return (
            roll(v, 1, 0) * x_gate,
            roll(v, 32, 1) * y_gate,
            jnp.where(depth_long == 0, roll(v, -31, 1), roll(v, 1, 1)) * z_lo,
        )

    def strip_above(v, gates):
        x_gate, y_gate, _, z_hi = gates
        return (
            roll(v * x_gate, -1, 0),
            roll(v * y_gate, -32, 1),
            jnp.where(depth_long == TILE - 1, roll(v, 31, 1), roll(v, -1, 1)) * z_hi,
        )

    def strip_velocity(v, p, m, gates, wanted):
        under = strip_below(p, gates)
        result = []
        for d in wanted:
            b, a = strip_below(v[d], gates), strip_above(v[d], gates)
            laplace = (b[0] + a[0]) + (b[1] + a[1]) + (b[2] + a[2]) - 6.0 * v[d]
            result.append(v[d] + RATE * m * (force_ref[d] + laplace - (p - under[d])))
        return result

    def strip_pressure(v, p, m, gates):
        total = zero_strip
        for d in range(3):
            total = total + (strip_above(v[d], gates)[d] - v[d])
        return p + PRESSURE_RATE * (m * total)

    zero_strip = jnp.zeros((PLANES, 128), f32)

    def put_lo(dst, v):
        dst[:, 0, :] = roll(v, 64, 1) * cross_lo

    def put_hi(dst, v):
        dst[:, 7, :] = roll(v, 96, 1) * cross_hi

    lo1 = strip_velocity(lo[:3], lo[3], lo[4], lo_gates, (0, 1, 2))
    hi1 = strip_velocity(hi[:3], hi[3], hi[4], hi_gates, (0, 1, 2))
    for d in range(3):
        put_lo(halo1.at[d], lo1[d])
        put_hi(halo1.at[d], hi1[d])
    lo_p1 = strip_pressure(lo1, lo[3], lo[4], lo_gates)
    hi_p1 = strip_pressure(hi1, hi[3], hi[4], hi_gates)
    put_lo(halo1.at[3], lo_p1)

    for x, step in ((-1, 2), (31, 3)):
        sub3, lane3 = iotas((step, 8, 128))
        velocity_planes(x, step, ext, ext.at[3], None, vel1)
    scale_lo, scale_hi = RATE * ext[4, :, 0, :], RATE * ext[4, :, 7, :]
    for d in range(3):
        face = lo[d] + lo[3] if d == 1 else lo[d]
        vel1[d, :, 0, :] = vel1[d, :, 0, :] + jnp.where(lane_long < 32, scale_lo * (roll(face, 96, 1) * cross_lo), 0.0)
        vel1[d, :, 7, :] = vel1[d, :, 7, :] + jnp.where(lane_long >= 96, scale_hi * (roll(hi[d], 64, 1) * cross_hi), 0.0)

    hear(1)
    tell(2, 4)
    tell(3, 1)

    step = 5
    sub3, lane3 = iotas((step, 8, 128))
    for x in range(-1, 32, step):
        pres1[planes(x, step)] = ext[3, planes(x, step)] + PRESSURE_RATE * divergence_planes(x, step, vel1, halo1.at[1])

    hi1 = [jnp.where(lane_long < 32, roll(vel1[d, :, 7, :], 32, 1), hi1[d]) for d in range(3)]
    hi_p1 = jnp.where(lane_long < 32, roll(pres1[:, 7, :], 32, 1), hi_p1)
    put_hi(halo2, strip_velocity(hi1, hi_p1, hi[4], hi_gates, (1,))[0])

    step = 3
    sub3, lane3 = iotas((step, 8, 128))
    for x in range(0, 33, step):
        velocity_planes(x, step, vel1, pres1, halo1, vel2)

    step = 8
    sub3, lane3 = iotas((step, 8, 128))
    message = zero
    for x in range(0, TILE, step):
        div = divergence_planes(x, step, vel2, halo2)
        pres2[pl.ds(x, step)] = pres1[planes(x, step)] + PRESSURE_RATE * div
        part = jnp.sum(div, axis=0)
        for shift in (1, 2, 4):
            part = part + jnp.where((lane // shift) % 2 == 0, roll(part, -shift, 1), roll(part, shift, 1))
        part = part + roll(part, 32, 1)
        part = part + roll(part, 64, 1)
        part = part + jnp.where(sub % 2 == 0, roll(part, -1, 0), roll(part, 1, 0))
        message = jnp.where(jnp.logical_and(2 * (lane // 32) + (lane % 8) // 4 == x // 8, sub == 2 * (lane % 4)), part, message)
    table[0, z_count // 2] = jnp.sum(message, axis=0, keepdims=True)[:, :64] * (1.0 / 64.0)

    hear(3)
    middle = z_count // 2
    near = []
    for k in range(1, NEAR + 1):
        for sign in (1, -1):
            index = len(near)
            near.append(pltpu.make_async_remote_copy(
                src_ref=table.at[0, middle], dst_ref=table.at[0, middle - sign * k], send_sem=gsend_sem.at[index], recv_sem=grecv_sem.at[index],
                device_id=along(0, sign * k), device_id_type=MESH))
    for copy in reversed(near):
        copy.start()

    stores = []
    for s in range(8):
        lanes = pl.ds(128 * s, 128)
        stores.append(pltpu.make_async_copy(vel2.at[:, pl.ds(OFF, TILE), s], fields_out.at[pl.ds(0, 3), :, lanes], store_sem.at[s]))
        stores.append(pltpu.make_async_copy(pres2.at[:, s], fields_out.at[3, :, lanes], store_sem.at[8 + s]))
    for copy in stores:
        copy.start()

    hear(2)
    tell(4, 3)
    hear(5)

    def copies(pairs):
        result = []
        for src, dst, device in pairs:
            index = next(counter)
            result.append(pltpu.make_async_remote_copy(
                src_ref=src, dst_ref=dst, send_sem=gsend_sem.at[index], recv_sem=grecv_sem.at[index], device_id=device, device_id_type=MESH))
            result[-1].start()
        return result

    counter = iter(range(len(near), GATHER_COPIES))
    for copy in near:
        copy.wait()
    hear(4)
    width = 2 * NEAR + 1
    block, below_block, above_block = pl.ds(middle - NEAR, width), pl.ds(0, width), pl.ds(2 * FAR, width)
    far = copies([(table.at[0, block], table.at[0, below_block], along(0, FAR)), (table.at[0, block], table.at[0, above_block], along(0, -FAR))])
    across = copies([(table.at[0, block], table.at[y_count - j, block], along(j, 0)) for j in range(1, y_count)])
    for copy in far:
        copy.wait()
    across += copies([(table.at[0, part], table.at[y_count - j, part], along(j, 0)) for j in range(1, y_count) for part in (below_block, above_block)])

    spot = lax.broadcasted_iota(jnp.int32, (64, 512), 1)
    entry = spot // 128 % 2 * 32 + spot % 4 * 8 + spot // 64 % 2 * 4 + spot // 8 % 4
    pick = jnp.where(lax.broadcasted_iota(jnp.int32, (64, 512), 0) == entry, 1.0, 0.0).astype(f32)
    spot = lax.broadcasted_iota(jnp.int32, (8, 512), 1)
    octant = spot // 256 * 4 + (spot // 32) % 2 * 2 + (spot // 4) % 2
    holds = lax.broadcasted_iota(jnp.int32, (8, 512), 0) == octant

    for copy in across:
        copy.wait()
    for o in range(8):
        source = source_ref[0, o]
        kept = jnp.maximum(source, 0)
        dy = lax.rem(kept // z_count - y + y_count, y_count)
        dz = lax.rem(lax.rem(kept, z_count) - z + z_count + middle, z_count)
        taken = table[dy, dz]
        row_buf[pl.ds(o, 1), :] = jnp.where(source >= 0, taken, jnp.zeros_like(taken))
    spread = jnp.dot(row_buf[...], pick, preferred_element_type=f32, precision=lax.Precision.HIGHEST)
    coarse_out[...] = jnp.sum(jnp.where(holds, spread, 0.0), axis=0, keepdims=True)

    for copy in stores:
        copy.wait()


def on_device(rows, fields, fluid_mask, body_force, neighbours, sources):
    y_count, z_count = 4, 32
    f32 = jnp.float32
    volume = lambda n: pltpu.VMEM((n, PLANES, 8, 128), f32)
    planes = lambda: pltpu.VMEM((PLANES, 8, 128), f32)
    any_space = pl.BlockSpec(memory_space=pl.ANY)
    hbm = pl.BlockSpec(memory_space=pltpu.HBM)
    new_fields, coarse = pl.pallas_call(
        functools.partial(kernel, rows, y_count, z_count),
        out_shape=(
            jax.ShapeDtypeStruct((4, TILE, TILE * TILE), f32),
            jax.ShapeDtypeStruct((1, 512), f32),
        ),
        in_specs=[hbm] * 5,
        out_specs=(any_space, pl.BlockSpec(memory_space=pltpu.VMEM)),
        scratch_shapes=[
            pltpu.SMEM((1, 6), jnp.int32),
            pltpu.SMEM((1, 8), jnp.int32),
            pltpu.SMEM((3,), f32),
            volume(6),
            pltpu.VMEM((TILE, 8, 128), jnp.int32),
            volume(3),
            planes(),
            volume(3),
            pltpu.VMEM((TILE, 8, 128), f32),
            volume(4),
            planes(),
            planes(),
            planes(),
            planes(),
            pltpu.VMEM((3, TILE, 128), f32),
            pltpu.VMEM((3, TILE, 128), f32),
            pltpu.VMEM((3, TILE, 128), f32),
            pltpu.VMEM((3, TILE, 128), f32),
            pltpu.VMEM((4, 8, 128), f32),
            pltpu.VMEM((4, 8, 128), f32),
            pltpu.VMEM((y_count, SLOTS, 1, 64), f32),
            pltpu.VMEM((8, 64), f32),
            pltpu.SemaphoreType.DMA((19,)),
            pltpu.SemaphoreType.DMA((16,)),
            pltpu.SemaphoreType.DMA((8,)),
            pltpu.SemaphoreType.DMA((8,)),
            pltpu.SemaphoreType.DMA((GATHER_COPIES,)),
            pltpu.SemaphoreType.DMA((GATHER_COPIES,)),
            pltpu.SemaphoreType.REGULAR((6,)),
        ],
        compiler_params=pltpu.CompilerParams(
            collective_id=0, has_side_effects=True, vmem_limit_bytes=32 * 1024 * 1024
        ),
    )(
        *(
            pltpu.with_memory_space_constraint(array, pltpu.HBM)
            for array in (
                neighbours,
                sources,
                body_force,
                fields.reshape(4, TILE, TILE * TILE),
                fluid_mask.reshape(TILE, TILE * TILE),
            )
        )
    )
    return new_fields[None], coarse


def solution(mesh):
    return jax.shard_map(
        functools.partial(on_device, mesh.shape["row"]),
        mesh=mesh,
        in_specs=(
            P(("row", "col"), None, None, None),
            P(("row", "col"), None, None),
            P(),
            P(("row", "col"), None),
            P(("row", "col"), None),
        ),
        out_specs=(P(("row", "col"), None, None, None), P(("row", "col"), None)),
        check_vma=False,
    )
```

```python
import functools

import jax
import jax.numpy as jnp
from jax import lax
from jax.experimental import pallas as pl
from jax.experimental.pallas import tpu as pltpu
from jax.sharding import PartitionSpec as P

MESH = pl.DeviceIdType.MESH
TILE = 32
RATE = 0.8 / 6.0
PRESSURE_RATE = 0.5
OFF = 8
PLANES = 48
NEAR = 5
FAR = 11
SLOTS = 33
GATHER_COPIES = 2 * NEAR + 2 + 9
DIRECT = 4


def roll(values, shift, axis):
    return pltpu.roll(values, shift % values.shape[axis], axis)


def kernel(
    rows, y_count, z_count,
    neighbour_hbm, source_hbm, force_hbm, fields_ref, mask_ref, fields_out, coarse_out,
    neighbour_ref, source_ref, force_ref,
    ext, mask_raw, vel1, pres1, vel2, pres2, halo1, halo2, gate_x, gate_lo, gate_hi,
    send_lo, send_hi, recv_lo, recv_hi, send_corner, recv_corner, table, straight, row_buf,
    load_sem, store_sem, send_sem, recv_sem, gsend_sem, grecv_sem, dsend_sem, drecv_sem, know_sem,
):
    f32 = jnp.float32
    cols = y_count * z_count
    r = lax.axis_index("row")
    c = lax.axis_index("col")
    y, z = c // z_count, lax.rem(c, z_count)

    def tile_at(dr, dc):
        return (lax.rem(r + dr + rows, rows), lax.rem(c + dc + cols, cols))

    def along(dy, dz):
        return (r, lax.rem(y + dy, y_count) * z_count + lax.rem(z + dz + z_count, z_count))

    greeted = [tile_at(dr, dc) for dr in (-1, 1) for dc in (-1, 1)]
    greeted += [tile_at(0, -1), tile_at(0, 1), tile_at(-1, 0), tile_at(1, 0)]
    greeted += [along(0, -1), along(0, 1), along(1, 0), along(y_count - 1, 0)]
    barrier = pltpu.get_barrier_semaphore()
    for device in greeted:
        pl.semaphore_signal(barrier, inc=1, device_id=device, device_id_type=MESH)
    is_direct = z < DIRECT
    is_late = jnp.logical_and(r == 0, c == 0)

    @pl.when(jnp.logical_and(is_direct, jnp.logical_not(is_late)))
    def _():
        def greet(k, carry):
            pl.semaphore_signal(barrier, inc=1, device_id=(r, lax.rem(c + k, cols)), device_id_type=MESH)
            return carry

        lax.fori_loop(1, cols, greet, 0)

    greetings = len(greeted) + y_count * DIRECT - jnp.where(jnp.logical_and(is_direct, jnp.logical_not(is_late)), 1, 0) - jnp.where(r == 0, 1, 0)

    smalls = [
        pltpu.make_async_copy(neighbour_hbm, neighbour_ref, load_sem.at[16]),
        pltpu.make_async_copy(source_hbm, source_ref, load_sem.at[17]),
        pltpu.make_async_copy(force_hbm, force_ref, load_sem.at[18]),
    ]
    for copy in smalls:
        copy.start()

    loads = []
    for s in range(8):
        lanes = pl.ds(128 * s, 128)
        loads.append(pltpu.make_async_copy(fields_ref.at[:, :, lanes], ext.at[pl.ds(0, 4), pl.ds(OFF, TILE), s], load_sem.at[s]))
        loads.append(pltpu.make_async_copy(mask_ref.at[:, lanes], mask_raw.at[:, s], load_sem.at[8 + s]))
    for copy in loads:
        copy.start()

    sub = lax.broadcasted_iota(jnp.int32, (8, 128), 0)
    lane = lax.broadcasted_iota(jnp.int32, (8, 128), 1)
    depth = lane % TILE
    lane_long = lax.broadcasted_iota(jnp.int32, (PLANES, 128), 1)
    zero = jnp.zeros((8, 128), f32)
    one = jnp.ones((8, 128), f32)

    for copy in smalls:
        copy.wait()

    def link(direction, exists):
        return jnp.where(jnp.logical_and(neighbour_ref[0, direction] == 0, exists), 1.0, 0.0).astype(f32)

    links = [link(0, r > 0), link(1, r < rows - 1), link(2, c > 0), link(3, c < cols - 1), link(4, True), link(5, True)]
    own = zero
    for d in range(6):
        own = jnp.where(sub == d, links[d], own)

    for x in (0, 1, 2, 30, 31):
        ext[5, OFF + x] = own

    def flag(tile, d):
        return jnp.broadcast_to(tile[d : d + 1, :], (8, 128))

    own_z_lo = jnp.where(depth == 0, flag(own, 4), one)
    own_z_hi = jnp.where(depth == TILE - 1, flag(own, 5), one)
    gate_x[...] = jnp.ones((PLANES, 8, 128), f32)
    gate_x[OFF] = flag(own, 0)
    gate_x[OFF + TILE] = flag(own, 1)
    gate_lo[pl.ds(OFF, TILE)] = jnp.broadcast_to(own_z_lo[None], (TILE, 8, 128))
    gate_hi[pl.ds(OFF, TILE)] = jnp.broadcast_to(own_z_hi[None], (TILE, 8, 128))

    for copy in loads:
        copy.wait()
    ext[4, pl.ds(OFF, TILE)] = mask_raw[...].astype(f32)

    lane_tile = lax.broadcasted_iota(jnp.int32, (TILE, 128), 1)
    flags_tile = jnp.concatenate([own] * 4, axis=0)
    top = [ext[f, pl.ds(OFF, TILE), 7, :] for f in range(5)]
    send_hi[0] = jnp.where(lane_tile >= 64, top[0], roll(top[1], 64, 1))
    send_hi[1] = jnp.where(lane_tile >= 64, top[2], roll(top[3], 64, 1))
    send_hi[2] = jnp.where(lane_tile >= 64, top[4], flags_tile)
    low = [ext[f, pl.ds(OFF, TILE), 0, :] for f in range(5)]
    send_lo[0] = jnp.where(lane_tile < 64, low[0], roll(low[2], 64, 1))
    send_lo[1] = jnp.where(lane_tile < 96, low[1], flags_tile)
    send_lo[2] = jnp.where(lane_tile < 64, low[3], roll(low[4], 64, 1))

    def corner(packed, x, up):
        tile = jnp.where(sub == 6, flag(own, 4), flag(own, 5))
        for g in range(3):
            tile = jnp.where(sub // 2 == g, roll(packed[g, x : x + 8], 2 * g - up, 0), tile)
        return tile

    send_corner[0] = corner(send_hi, 24, 6)
    send_corner[1] = corner(send_hi, 0, 0)
    send_corner[2] = corner(send_lo, 24, 6)
    send_corner[3] = corner(send_lo, 0, 0)

    pl.semaphore_wait(barrier, greetings)

    plan = [(send_corner.at[k], recv_corner.at[k], offset) for k, offset in enumerate([(1, 1), (-1, 1), (1, -1), (-1, -1)])]
    plan += [(send_hi, recv_lo, (0, 1)), (send_lo, recv_hi, (0, -1))]
    faces = []
    for k, (src, dst, offset) in enumerate(plan):
        faces.append(pltpu.make_async_remote_copy(
            src_ref=src, dst_ref=dst, send_sem=send_sem.at[k], recv_sem=recv_sem.at[k], device_id=tile_at(*offset), device_id_type=MESH))
    faces.append(pltpu.make_async_remote_copy(
        src_ref=ext.at[:, pl.ds(OFF + 30, 2)], dst_ref=ext.at[:, pl.ds(OFF - 2, 2)], send_sem=send_sem.at[6], recv_sem=recv_sem.at[6],
        device_id=tile_at(1, 0), device_id_type=MESH))
    faces.append(pltpu.make_async_remote_copy(
        src_ref=ext.at[:, pl.ds(OFF, 3)], dst_ref=ext.at[:, pl.ds(OFF + TILE, 3)], send_sem=send_sem.at[7], recv_sem=recv_sem.at[7],
        device_id=tile_at(-1, 0), device_id_type=MESH))
    for copy in faces:
        copy.start()

    def tell(step, reach):
        for device in (along(0, reach), along(0, -reach)):
            pl.semaphore_signal(know_sem.at[step], inc=1, device_id=device, device_id_type=MESH)

    def hear(step):
        pl.semaphore_wait(know_sem.at[step], 2)

    tell(0, 1)
    for j in (1, y_count - 1):
        pl.semaphore_signal(know_sem.at[5], inc=1, device_id=along(j, 0), device_id_type=MESH)

    def iotas(shape):
        return lax.broadcasted_iota(jnp.int32, shape, 1), lax.broadcasted_iota(jnp.int32, shape, 2)

    def below_y(v, h):
        w = jnp.where(sub3 == 0, 0.0 if h is None else h, roll(v, 1, 1))
        return roll(jnp.where(lane3 >= 96, w, v), 32, 2)

    def above_y(v, h):
        w = jnp.where(sub3 == 7, 0.0 if h is None else h, roll(v, -1, 1))
        return roll(jnp.where(lane3 < 32, w, v), -32, 2)

    def below_z(v, g):
        return jnp.where(lane3 % TILE == 0, roll(v, -31, 2), roll(v, 1, 2)) * g

    def above_z(v, g):
        return jnp.where(lane3 % TILE == TILE - 1, roll(v, 31, 2), roll(v, -1, 2)) * g

    def planes(x, n):
        return pl.ds(OFF + x, n)

    def velocity_planes(x, n, v_in, p_in, halo, v_out):
        here, under, over = planes(x, n), planes(x - 1, n), planes(x + 1, n)
        g_under, g_over, g_lo, g_hi = gate_x[here], gate_x[over], gate_lo[here], gate_hi[here]
        scale = RATE * ext[4, here]
        p = p_in[here]
        p_below = (p_in[under] * g_under, below_y(p, None if halo is None else halo[3, here]), below_z(p, g_lo))
        for d in range(3):
            v, h = v_in[d, here], None if halo is None else halo[d, here]
            total = (v_in[d, under] * g_under + v_in[d, over] * g_over) + (below_y(v, h) + above_y(v, h))
            total = total + (below_z(v, g_lo) + above_z(v, g_hi)) - 6.0 * v
            v_out[d, here] = v + scale * (force_ref[d] + total - (p - p_below[d]))

    def divergence_planes(x, n, v_in, halo_y):
        here, over = planes(x, n), planes(x + 1, n)
        vx, vy, vz = v_in[0, here], v_in[1, here], v_in[2, here]
        total = (v_in[0, over] * gate_x[over] - vx) + (above_y(vy, halo_y[here]) - vy) + (above_z(vz, gate_hi[here]) - vz)
        return ext[4, here] * total

    step, shape3 = 5, (5, 8, 128)
    sub3, lane3 = iotas(shape3)
    for x in range(1, 31, step):
        velocity_planes(x, step, ext, ext.at[3], None, vel1)
        if x == 1:
            hear(0)
            tell(1, 2)

    for copy in faces:
        copy.wait()

    row_lo, row_hi = ext[5, OFF - 1], ext[5, OFF + TILE]

    def spread_lo(tile):
        return jnp.where(lane < 64, tile, roll(tile, 64, 1))

    def spread_hi(tile):
        half = jnp.where(lane >= 96, tile, roll(tile, 96, 1))
        return jnp.where(lane >= 64, half, roll(half, 64, 1))

    corners = [recv_corner[k] for k in range(4)]
    col_lo, col_hi = spread_lo(recv_lo[2, 0:8]), spread_hi(recv_hi[1, 0:8])
    z_lo_outer = [(flag(corners[k], 6), flag(col, 4), flag(corners[k + 1], 6)) for k, col in ((0, col_lo), (2, col_hi))]
    z_hi_outer = [(flag(corners[k], 7), flag(col, 5), flag(corners[k + 1], 7)) for k, col in ((0, col_lo), (2, col_hi))]
    mid = [row_lo, own, row_hi]
    for k, x, n in ((0, OFF - 2, 2), (2, OFF + TILE, 3)):
        gate_lo[pl.ds(x, n)] = jnp.broadcast_to(jnp.where(depth == 0, flag(mid[k], 4), one)[None], (n, 8, 128))
        gate_hi[pl.ds(x, n)] = jnp.broadcast_to(jnp.where(depth == TILE - 1, flag(mid[k], 5), one)[None], (n, 8, 128))

    def by_region(tiles):
        return jnp.concatenate([tiles[0]] + [tiles[1]] * 4 + [tiles[2]], axis=0)

    def strip_gates(side, col, is_own, crossing, d):
        z_lo, z_hi, cross = [], [], []
        for k in range(3):
            z_lo.append(jnp.where(depth == 0, jnp.where(is_own, flag(mid[k], 4), z_lo_outer[side][k]), one))
            z_hi.append(jnp.where(depth == TILE - 1, jnp.where(is_own, flag(mid[k], 5), z_hi_outer[side][k]), one))
            cross.append(jnp.where(crossing, flag(mid[k], d), one))
        x_lo = jnp.where(sub == 0, jnp.where(is_own, flag(own, 0), flag(col, 0)), one)
        x_hi = jnp.where(sub == 0, jnp.where(is_own, flag(own, 1), flag(col, 1)), one)
        x_gate = jnp.concatenate([one, x_lo, one, one, one, x_hi], axis=0)
        return x_gate, by_region(cross), by_region(z_lo), by_region(z_hi)

    lo_gates = strip_gates(0, col_lo, lane >= 64, lane // TILE == 2, 2)
    hi_gates = strip_gates(1, col_hi, lane < 32, lane // TILE == 1, 3)
    cross_lo = by_region([flag(tile, 2) for tile in mid])
    cross_hi = by_region([flag(tile, 3) for tile in mid])

    def strip(received, tiles, g):
        return jnp.concatenate([roll(tiles[0], 6 - 2 * g, 0), received[g], roll(tiles[1], -2 * g, 0)], axis=0)

    raw = [strip(recv_lo, corners[:2], g) for g in range(3)]
    outer = [roll(raw[0], 64, 1), raw[0], roll(raw[1], 64, 1), raw[1], roll(raw[2], 64, 1)]
    lo = [jnp.where(lane_long < 64, outer[f], roll(ext[f, :, 0, :], 64, 1)) for f in range(5)]
    raw = [strip(recv_hi, corners[2:], g) for g in range(3)]
    outer = [roll(raw[0], 32, 1), roll(raw[1], 32, 1), roll(raw[0], 96, 1), roll(raw[2], 32, 1), roll(raw[2], 96, 1)]
    hi = [jnp.where(lane_long < 32, roll(ext[f, :, 7, :], 32, 1), outer[f]) for f in range(5)]

    depth_long = lane_long % TILE

    def strip_below(v, gates):
        x_gate, y_gate, z_lo, _ = gates
        return (
            roll(v, 1, 0) * x_gate,
            roll(v, 32, 1) * y_gate,
            jnp.where(depth_long == 0, roll(v, -31, 1), roll(v, 1, 1)) * z_lo,
        )

    def strip_above(v, gates):
        x_gate, y_gate, _, z_hi = gates
        return (
            roll(v * x_gate, -1, 0),
            roll(v * y_gate, -32, 1),
            jnp.where(depth_long == TILE - 1, roll(v, 31, 1), roll(v, -1, 1)) * z_hi,
        )

    def strip_velocity(v, p, m, gates, wanted):
        under = strip_below(p, gates)
        result = []
        for d in wanted:
            b, a = strip_below(v[d], gates), strip_above(v[d], gates)
            laplace = (b[0] + a[0]) + (b[1] + a[1]) + (b[2] + a[2]) - 6.0 * v[d]
            result.append(v[d] + RATE * m * (force_ref[d] + laplace - (p - under[d])))
        return result

    def strip_pressure(v, p, m, gates):
        total = zero_strip
        for d in range(3):
            total = total + (strip_above(v[d], gates)[d] - v[d])
        return p + PRESSURE_RATE * (m * total)

    zero_strip = jnp.zeros((PLANES, 128), f32)

    def put_lo(dst, v):
        dst[:, 0, :] = roll(v, 64, 1) * cross_lo

    def put_hi(dst, v):
        dst[:, 7, :] = roll(v, 96, 1) * cross_hi

    lo1 = strip_velocity(lo[:3], lo[3], lo[4], lo_gates, (0, 1, 2))
    hi1 = strip_velocity(hi[:3], hi[3], hi[4], hi_gates, (0, 1, 2))
    for d in range(3):
        put_lo(halo1.at[d], lo1[d])
        put_hi(halo1.at[d], hi1[d])
    lo_p1 = strip_pressure(lo1, lo[3], lo[4], lo_gates)
    hi_p1 = strip_pressure(hi1, hi[3], hi[4], hi_gates)
    put_lo(halo1.at[3], lo_p1)

    for x, step in ((-1, 2), (31, 3)):
        sub3, lane3 = iotas((step, 8, 128))
        velocity_planes(x, step, ext, ext.at[3], None, vel1)
    scale_lo, scale_hi = RATE * ext[4, :, 0, :], RATE * ext[4, :, 7, :]
    for d in range(3):
        face = lo[d] + lo[3] if d == 1 else lo[d]
        vel1[d, :, 0, :] = vel1[d, :, 0, :] + jnp.where(lane_long < 32, scale_lo * (roll(face, 96, 1) * cross_lo), 0.0)
        vel1[d, :, 7, :] = vel1[d, :, 7, :] + jnp.where(lane_long >= 96, scale_hi * (roll(hi[d], 64, 1) * cross_hi), 0.0)

    hear(1)
    tell(2, 4)
    tell(3, 1)

    step = 5
    sub3, lane3 = iotas((step, 8, 128))
    for x in range(-1, 32, step):
        pres1[planes(x, step)] = ext[3, planes(x, step)] + PRESSURE_RATE * divergence_planes(x, step, vel1, halo1.at[1])

    hi1 = [jnp.where(lane_long < 32, roll(vel1[d, :, 7, :], 32, 1), hi1[d]) for d in range(3)]
    hi_p1 = jnp.where(lane_long < 32, roll(pres1[:, 7, :], 32, 1), hi_p1)
    put_hi(halo2, strip_velocity(hi1, hi_p1, hi[4], hi_gates, (1,))[0])

    step = 3
    sub3, lane3 = iotas((step, 8, 128))
    for x in range(0, 33, step):
        velocity_planes(x, step, vel1, pres1, halo1, vel2)

    step = 8
    sub3, lane3 = iotas((step, 8, 128))
    message = zero
    for x in range(0, TILE, step):
        div = divergence_planes(x, step, vel2, halo2)
        pres2[pl.ds(x, step)] = pres1[planes(x, step)] + PRESSURE_RATE * div
        part = jnp.sum(div, axis=0)
        for shift in (1, 2, 4):
            part = part + jnp.where((lane // shift) % 2 == 0, roll(part, -shift, 1), roll(part, shift, 1))
        part = part + roll(part, 32, 1)
        part = part + roll(part, 64, 1)
        part = part + jnp.where(sub % 2 == 0, roll(part, -1, 0), roll(part, 1, 0))
        message = jnp.where(jnp.logical_and(2 * (lane // 32) + (lane % 8) // 4 == x // 8, sub == 2 * (lane % 4)), part, message)
    table[0, z_count // 2] = jnp.sum(message, axis=0, keepdims=True)[:, :64] * (1.0 / 64.0)

    middle = z_count // 2

    def straight_copy(dy, at):
        return pltpu.make_async_remote_copy(
            src_ref=table.at[0, pl.ds(middle, 1)], dst_ref=straight.at[pl.ds(c, 1)], send_sem=dsend_sem.at[dy * DIRECT + at], recv_sem=drecv_sem.at[0],
            device_id=(r, lax.rem(y + dy, y_count) * z_count + at), device_id_type=MESH)

    def straight_goes(dy, at):
        goes = z != at if dy == 0 else None
        if at == 0:
            awake = jnp.logical_or(r > 0, lax.rem(y + dy, y_count) > 0)
            goes = awake if goes is None else jnp.logical_and(goes, awake)
        return goes

    def for_each_straight(act):
        for dy in (2, 1, y_count - 1, 0):
            for at in range(DIRECT):
                goes = straight_goes(dy, at)
                if goes is None:
                    act(straight_copy(dy, at))
                else:
                    pl.when(goes)(functools.partial(act, straight_copy(dy, at)))

    for_each_straight(lambda copy: copy.start())

    hear(3)
    near = []
    for k in range(1, NEAR + 1):
        for sign in (1, -1):
            index = len(near)
            near.append(pltpu.make_async_remote_copy(
                src_ref=table.at[0, middle], dst_ref=table.at[0, middle - sign * k], send_sem=gsend_sem.at[index], recv_sem=grecv_sem.at[index],
                device_id=along(0, sign * k), device_id_type=MESH))
    for copy in reversed(near):
        copy.start()

    stores = []
    for s in range(8):
        lanes = pl.ds(128 * s, 128)
        stores.append(pltpu.make_async_copy(vel2.at[:, pl.ds(OFF, TILE), s], fields_out.at[pl.ds(0, 3), :, lanes], store_sem.at[s]))
        stores.append(pltpu.make_async_copy(pres2.at[:, s], fields_out.at[3, :, lanes], store_sem.at[8 + s]))
    for copy in stores:
        copy.start()

    hear(2)
    tell(4, 3)
    hear(5)

    for copy in near:
        copy.wait()
    hear(4)
    width = 2 * NEAR + 1
    block, below_block, above_block = pl.ds(middle - NEAR, width), pl.ds(0, width), pl.ds(2 * FAR, width)
    far = []
    for k, (sign, landed) in enumerate(((1, below_block), (-1, above_block))):
        far.append(pltpu.make_async_remote_copy(
            src_ref=table.at[0, block], dst_ref=table.at[0, landed], send_sem=gsend_sem.at[len(near) + k], recv_sem=grecv_sem.at[len(near) + k],
            device_id=along(0, sign * FAR), device_id_type=MESH))
    wanted = [lax.rem(z + sign * FAR + z_count, z_count) >= DIRECT for sign in (1, -1)]
    for copy, needed in zip(far, wanted, strict=True):
        pl.when(needed)(copy.start)

    def y_copies(parts, first):
        result = []
        for j in range(1, y_count):
            for part in parts:
                index = first + len(result)
                result.append(pltpu.make_async_remote_copy(
                    src_ref=table.at[0, part], dst_ref=table.at[y_count - j, part], send_sem=gsend_sem.at[index], recv_sem=grecv_sem.at[index],
                    device_id=along(j, 0), device_id_type=MESH))
        return result

    across = y_copies([block], len(near) + 2)
    across_far = y_copies([below_block, above_block], len(near) + 2 + len(across))

    @pl.when(jnp.logical_not(is_direct))
    def _():
        for copy in across:
            copy.start()
        for copy in far:
            copy.wait_recv()
        for copy in across_far:
            copy.start()

    spot = lax.broadcasted_iota(jnp.int32, (64, 512), 1)
    entry = spot // 128 % 2 * 32 + spot % 4 * 8 + spot // 64 % 2 * 4 + spot // 8 % 4
    pick = jnp.where(lax.broadcasted_iota(jnp.int32, (64, 512), 0) == entry, 1.0, 0.0).astype(f32)
    spot = lax.broadcasted_iota(jnp.int32, (8, 512), 1)
    octant = spot // 256 * 4 + (spot // 32) % 2 * 2 + (spot // 4) % 2
    holds = lax.broadcasted_iota(jnp.int32, (8, 512), 0) == octant

    for copy, needed in zip(far, wanted, strict=True):
        pl.when(needed)(copy.wait_send)
    for_each_straight(lambda copy: copy.wait_send())

    sources = [source_ref[0, o] for o in range(8)]
    kept = [jnp.maximum(source, 0) for source in sources]

    def keep(o, taken):
        row_buf[pl.ds(o, 1), :] = jnp.where(sources[o] >= 0, taken, jnp.zeros_like(taken))

    handed = pltpu.make_async_remote_copy(
        src_ref=straight, dst_ref=straight, send_sem=dsend_sem.at[y_count * DIRECT], recv_sem=drecv_sem.at[1], device_id=(r, 0 * c), device_id_type=MESH)
    hands_on = jnp.logical_and(r == 0, c == 1)

    @pl.when(jnp.logical_and(is_direct, jnp.logical_not(is_late)))
    def _():
        straight[pl.ds(c, 1)] = table[0, pl.ds(middle, 1)]
        arrived = straight.at[pl.ds(0, cols - 1)]
        pltpu.make_async_copy(arrived, arrived, drecv_sem.at[0]).wait()

    pl.when(hands_on)(handed.start)
    pl.when(is_late)(handed.wait_recv)

    @pl.when(is_direct)
    def _():
        for o in range(8):
            keep(o, straight[kept[o]])

    @pl.when(jnp.logical_not(is_direct))
    def _():
        for copy in across + across_far:
            copy.wait()
        for o in range(8):
            dy = lax.rem(kept[o] // z_count - y + y_count, y_count)
            dz = lax.rem(lax.rem(kept[o], z_count) - z + z_count + middle, z_count)
            keep(o, table[dy, dz])

    spread = jnp.dot(row_buf[...], pick, preferred_element_type=f32, precision=lax.Precision.HIGHEST)
    coarse_out[...] = jnp.sum(jnp.where(holds, spread, 0.0), axis=0, keepdims=True)

    for copy in stores:
        copy.wait()
    pl.when(hands_on)(handed.wait_send)


def on_device(rows, fields, fluid_mask, body_force, neighbours, sources):
    y_count, z_count = 4, 32
    f32 = jnp.float32
    volume = lambda n: pltpu.VMEM((n, PLANES, 8, 128), f32)
    planes = lambda: pltpu.VMEM((PLANES, 8, 128), f32)
    any_space = pl.BlockSpec(memory_space=pl.ANY)
    hbm = pl.BlockSpec(memory_space=pltpu.HBM)
    new_fields, coarse = pl.pallas_call(
        functools.partial(kernel, rows, y_count, z_count),
        out_shape=(
            jax.ShapeDtypeStruct((4, TILE, TILE * TILE), f32),
            jax.ShapeDtypeStruct((1, 512), f32),
        ),
        in_specs=[hbm] * 5,
        out_specs=(any_space, pl.BlockSpec(memory_space=pltpu.VMEM)),
        scratch_shapes=[
            pltpu.SMEM((1, 6), jnp.int32),
            pltpu.SMEM((1, 8), jnp.int32),
            pltpu.SMEM((3,), f32),
            volume(6),
            pltpu.VMEM((TILE, 8, 128), jnp.int32),
            volume(3),
            planes(),
            volume(3),
            pltpu.VMEM((TILE, 8, 128), f32),
            volume(4),
            planes(),
            planes(),
            planes(),
            planes(),
            pltpu.VMEM((3, TILE, 128), f32),
            pltpu.VMEM((3, TILE, 128), f32),
            pltpu.VMEM((3, TILE, 128), f32),
            pltpu.VMEM((3, TILE, 128), f32),
            pltpu.VMEM((4, 8, 128), f32),
            pltpu.VMEM((4, 8, 128), f32),
            pltpu.VMEM((y_count, SLOTS, 1, 64), f32),
            pltpu.VMEM((y_count * z_count, 1, 64), f32),
            pltpu.VMEM((8, 64), f32),
            pltpu.SemaphoreType.DMA((19,)),
            pltpu.SemaphoreType.DMA((16,)),
            pltpu.SemaphoreType.DMA((8,)),
            pltpu.SemaphoreType.DMA((8,)),
            pltpu.SemaphoreType.DMA((GATHER_COPIES,)),
            pltpu.SemaphoreType.DMA((GATHER_COPIES,)),
            pltpu.SemaphoreType.DMA((y_count * DIRECT + 1,)),
            pltpu.SemaphoreType.DMA((2,)),
            pltpu.SemaphoreType.REGULAR((6,)),
        ],
        compiler_params=pltpu.CompilerParams(
            collective_id=0, has_side_effects=True, vmem_limit_bytes=32 * 1024 * 1024
        ),
    )(
        *(
            pltpu.with_memory_space_constraint(array, pltpu.HBM)
            for array in (
                neighbours,
                sources,
                body_force,
                fields.reshape(4, TILE, TILE * TILE),
                fluid_mask.reshape(TILE, TILE * TILE),
            )
        )
    )
    return new_fields[None], coarse


def solution(mesh):
    return jax.shard_map(
        functools.partial(on_device, mesh.shape["row"]),
        mesh=mesh,
        in_specs=(
            P(("row", "col"), None, None, None),
            P(("row", "col"), None, None),
            P(),
            P(("row", "col"), None),
            P(("row", "col"), None),
        ),
        out_specs=(P(("row", "col"), None, None, None), P(("row", "col"), None)),
        check_vma=False,
    )
```

```python
import functools

import jax
import jax.numpy as jnp
from jax import lax
from jax.experimental import pallas as pl
from jax.experimental.pallas import tpu as pltpu
from jax.sharding import PartitionSpec as P

MESH = pl.DeviceIdType.MESH
TILE = 32
RATE = 0.8 / 6.0
PRESSURE_RATE = 0.5
OFF = 8
PLANES = 48
NEAR = 5
FAR = 11
SLOTS = 33
GATHER_COPIES = 2 * NEAR + 2 + 9
DIRECT = 4
MID = 7


def roll(values, shift, axis):
    return pltpu.roll(values, shift % values.shape[axis], axis)


def kernel(
    rows, y_count, z_count,
    neighbour_hbm, source_hbm, force_hbm, fields_ref, mask_ref, fields_out, coarse_out,
    neighbour_ref, source_ref, force_ref,
    ext, mask_raw, vel1, pres1, vel2, pres2, halo1, halo2, gate_x, gate_lo, gate_hi,
    send_lo, send_hi, recv_lo, recv_hi, send_corner, recv_corner, table, straight, row_buf,
    load_sem, store_sem, send_sem, recv_sem, gsend_sem, grecv_sem, dsend_sem, drecv_sem, know_sem,
):
    f32 = jnp.float32
    cols = y_count * z_count
    r = lax.axis_index("row")
    c = lax.axis_index("col")
    y, z = c // z_count, lax.rem(c, z_count)

    def tile_at(dr, dc):
        return (lax.rem(r + dr + rows, rows), lax.rem(c + dc + cols, cols))

    def along(dy, dz):
        return (r, lax.rem(y + dy, y_count) * z_count + lax.rem(z + dz + z_count, z_count))

    greeted = [tile_at(dr, dc) for dr in (-1, 1) for dc in (-1, 1)]
    greeted += [tile_at(0, -1), tile_at(0, 1), tile_at(-1, 0), tile_at(1, 0)]
    greeted += [along(0, -1), along(0, 1), along(1, 0), along(y_count - 1, 0)]
    barrier = pltpu.get_barrier_semaphore()
    for device in greeted:
        pl.semaphore_signal(barrier, inc=1, device_id=device, device_id_type=MESH)
    is_direct = z < DIRECT
    is_late = jnp.logical_and(r == 0, c == 0)

    @pl.when(jnp.logical_and(is_direct, jnp.logical_not(is_late)))
    def _():
        def greet(k, carry):
            pl.semaphore_signal(barrier, inc=1, device_id=(r, lax.rem(c + k, cols)), device_id_type=MESH)
            return carry

        lax.fori_loop(1, cols, greet, 0)

    is_mid = jnp.logical_and(z >= DIRECT, z < MID)

    @pl.when(is_mid)
    def _():
        def greet(k, carry):
            pl.semaphore_signal(barrier, inc=1, device_id=(r, y * z_count + lax.rem(z + k, z_count)), device_id_type=MESH)
            return carry

        lax.fori_loop(1, z_count, greet, 0)

    greetings = len(greeted) + y_count * DIRECT - jnp.where(jnp.logical_and(is_direct, jnp.logical_not(is_late)), 1, 0) - jnp.where(r == 0, 1, 0) + MID - DIRECT - jnp.where(is_mid, 1, 0)

    smalls = [
        pltpu.make_async_copy(neighbour_hbm, neighbour_ref, load_sem.at[16]),
        pltpu.make_async_copy(source_hbm, source_ref, load_sem.at[17]),
        pltpu.make_async_copy(force_hbm, force_ref, load_sem.at[18]),
    ]
    for copy in smalls:
        copy.start()

    loads = []
    for s in range(8):
        lanes = pl.ds(128 * s, 128)
        loads.append(pltpu.make_async_copy(fields_ref.at[:, :, lanes], ext.at[pl.ds(0, 4), pl.ds(OFF, TILE), s], load_sem.at[s]))
        loads.append(pltpu.make_async_copy(mask_ref.at[:, lanes], mask_raw.at[:, s], load_sem.at[8 + s]))
    for copy in loads:
        copy.start()

    sub = lax.broadcasted_iota(jnp.int32, (8, 128), 0)
    lane = lax.broadcasted_iota(jnp.int32, (8, 128), 1)
    depth = lane % TILE
    lane_long = lax.broadcasted_iota(jnp.int32, (PLANES, 128), 1)
    zero = jnp.zeros((8, 128), f32)
    one = jnp.ones((8, 128), f32)

    for copy in smalls:
        copy.wait()

    def link(direction, exists):
        return jnp.where(jnp.logical_and(neighbour_ref[0, direction] == 0, exists), 1.0, 0.0).astype(f32)

    links = [link(0, r > 0), link(1, r < rows - 1), link(2, c > 0), link(3, c < cols - 1), link(4, True), link(5, True)]
    own = zero
    for d in range(6):
        own = jnp.where(sub == d, links[d], own)

    for x in (0, 1, 2, 30, 31):
        ext[5, OFF + x] = own

    def flag(tile, d):
        return jnp.broadcast_to(tile[d : d + 1, :], (8, 128))

    own_z_lo = jnp.where(depth == 0, flag(own, 4), one)
    own_z_hi = jnp.where(depth == TILE - 1, flag(own, 5), one)
    gate_x[...] = jnp.ones((PLANES, 8, 128), f32)
    gate_x[OFF] = flag(own, 0)
    gate_x[OFF + TILE] = flag(own, 1)
    gate_lo[pl.ds(OFF, TILE)] = jnp.broadcast_to(own_z_lo[None], (TILE, 8, 128))
    gate_hi[pl.ds(OFF, TILE)] = jnp.broadcast_to(own_z_hi[None], (TILE, 8, 128))

    for copy in loads:
        copy.wait()
    ext[4, pl.ds(OFF, TILE)] = mask_raw[...].astype(f32)

    lane_tile = lax.broadcasted_iota(jnp.int32, (TILE, 128), 1)
    flags_tile = jnp.concatenate([own] * 4, axis=0)
    top = [ext[f, pl.ds(OFF, TILE), 7, :] for f in range(5)]
    send_hi[0] = jnp.where(lane_tile >= 64, top[0], roll(top[1], 64, 1))
    send_hi[1] = jnp.where(lane_tile >= 64, top[2], roll(top[3], 64, 1))
    send_hi[2] = jnp.where(lane_tile >= 64, top[4], flags_tile)
    low = [ext[f, pl.ds(OFF, TILE), 0, :] for f in range(5)]
    send_lo[0] = jnp.where(lane_tile < 64, low[0], roll(low[2], 64, 1))
    send_lo[1] = jnp.where(lane_tile < 96, low[1], flags_tile)
    send_lo[2] = jnp.where(lane_tile < 64, low[3], roll(low[4], 64, 1))

    def corner(packed, x, up):
        tile = jnp.where(sub == 6, flag(own, 4), flag(own, 5))
        for g in range(3):
            tile = jnp.where(sub // 2 == g, roll(packed[g, x : x + 8], 2 * g - up, 0), tile)
        return tile

    send_corner[0] = corner(send_hi, 24, 6)
    send_corner[1] = corner(send_hi, 0, 0)
    send_corner[2] = corner(send_lo, 24, 6)
    send_corner[3] = corner(send_lo, 0, 0)

    pl.semaphore_wait(barrier, greetings)

    plan = [(send_corner.at[k], recv_corner.at[k], offset) for k, offset in enumerate([(1, 1), (-1, 1), (1, -1), (-1, -1)])]
    plan += [(send_hi, recv_lo, (0, 1)), (send_lo, recv_hi, (0, -1))]
    faces = []
    for k, (src, dst, offset) in enumerate(plan):
        faces.append(pltpu.make_async_remote_copy(
            src_ref=src, dst_ref=dst, send_sem=send_sem.at[k], recv_sem=recv_sem.at[k], device_id=tile_at(*offset), device_id_type=MESH))
    faces.append(pltpu.make_async_remote_copy(
        src_ref=ext.at[:, pl.ds(OFF + 30, 2)], dst_ref=ext.at[:, pl.ds(OFF - 2, 2)], send_sem=send_sem.at[6], recv_sem=recv_sem.at[6],
        device_id=tile_at(1, 0), device_id_type=MESH))
    faces.append(pltpu.make_async_remote_copy(
        src_ref=ext.at[:, pl.ds(OFF, 3)], dst_ref=ext.at[:, pl.ds(OFF + TILE, 3)], send_sem=send_sem.at[7], recv_sem=recv_sem.at[7],
        device_id=tile_at(-1, 0), device_id_type=MESH))
    for copy in faces:
        copy.start()

    def tell(step, reach):
        for device in (along(0, reach), along(0, -reach)):
            pl.semaphore_signal(know_sem.at[step], inc=1, device_id=device, device_id_type=MESH)

    def hear(step):
        pl.semaphore_wait(know_sem.at[step], 2)

    tell(0, 1)
    for j in (1, y_count - 1):
        pl.semaphore_signal(know_sem.at[5], inc=1, device_id=along(j, 0), device_id_type=MESH)

    def iotas(shape):
        return lax.broadcasted_iota(jnp.int32, shape, 1), lax.broadcasted_iota(jnp.int32, shape, 2)

    def below_y(v, h):
        w = jnp.where(sub3 == 0, 0.0 if h is None else h, roll(v, 1, 1))
        return roll(jnp.where(lane3 >= 96, w, v), 32, 2)

    def above_y(v, h):
        w = jnp.where(sub3 == 7, 0.0 if h is None else h, roll(v, -1, 1))
        return roll(jnp.where(lane3 < 32, w, v), -32, 2)

    def below_z(v, g):
        return jnp.where(lane3 % TILE == 0, roll(v, -31, 2), roll(v, 1, 2)) * g

    def above_z(v, g):
        return jnp.where(lane3 % TILE == TILE - 1, roll(v, 31, 2), roll(v, -1, 2)) * g

    def planes(x, n):
        return pl.ds(OFF + x, n)

    def velocity_planes(x, n, v_in, p_in, halo, v_out):
        here, under, over = planes(x, n), planes(x - 1, n), planes(x + 1, n)
        g_under, g_over, g_lo, g_hi = gate_x[here], gate_x[over], gate_lo[here], gate_hi[here]
        scale = RATE * ext[4, here]
        p = p_in[here]
        p_below = (p_in[under] * g_under, below_y(p, None if halo is None else halo[3, here]), below_z(p, g_lo))
        for d in range(3):
            v, h = v_in[d, here], None if halo is None else halo[d, here]
            total = (v_in[d, under] * g_under + v_in[d, over] * g_over) + (below_y(v, h) + above_y(v, h))
            total = total + (below_z(v, g_lo) + above_z(v, g_hi)) - 6.0 * v
            v_out[d, here] = v + scale * (force_ref[d] + total - (p - p_below[d]))

    def divergence_planes(x, n, v_in, halo_y):
        here, over = planes(x, n), planes(x + 1, n)
        vx, vy, vz = v_in[0, here], v_in[1, here], v_in[2, here]
        total = (v_in[0, over] * gate_x[over] - vx) + (above_y(vy, halo_y[here]) - vy) + (above_z(vz, gate_hi[here]) - vz)
        return ext[4, here] * total

    step, shape3 = 5, (5, 8, 128)
    sub3, lane3 = iotas(shape3)
    for x in range(1, 31, step):
        velocity_planes(x, step, ext, ext.at[3], None, vel1)
        if x == 1:
            hear(0)
            tell(1, 2)

    for copy in faces:
        copy.wait()

    row_lo, row_hi = ext[5, OFF - 1], ext[5, OFF + TILE]

    def spread_lo(tile):
        return jnp.where(lane < 64, tile, roll(tile, 64, 1))

    def spread_hi(tile):
        half = jnp.where(lane >= 96, tile, roll(tile, 96, 1))
        return jnp.where(lane >= 64, half, roll(half, 64, 1))

    corners = [recv_corner[k] for k in range(4)]
    col_lo, col_hi = spread_lo(recv_lo[2, 0:8]), spread_hi(recv_hi[1, 0:8])
    z_lo_outer = [(flag(corners[k], 6), flag(col, 4), flag(corners[k + 1], 6)) for k, col in ((0, col_lo), (2, col_hi))]
    z_hi_outer = [(flag(corners[k], 7), flag(col, 5), flag(corners[k + 1], 7)) for k, col in ((0, col_lo), (2, col_hi))]
    mid = [row_lo, own, row_hi]
    for k, x, n in ((0, OFF - 2, 2), (2, OFF + TILE, 3)):
        gate_lo[pl.ds(x, n)] = jnp.broadcast_to(jnp.where(depth == 0, flag(mid[k], 4), one)[None], (n, 8, 128))
        gate_hi[pl.ds(x, n)] = jnp.broadcast_to(jnp.where(depth == TILE - 1, flag(mid[k], 5), one)[None], (n, 8, 128))

    def by_region(tiles):
        return jnp.concatenate([tiles[0]] + [tiles[1]] * 4 + [tiles[2]], axis=0)

    def strip_gates(side, col, is_own, crossing, d):
        z_lo, z_hi, cross = [], [], []
        for k in range(3):
            z_lo.append(jnp.where(depth == 0, jnp.where(is_own, flag(mid[k], 4), z_lo_outer[side][k]), one))
            z_hi.append(jnp.where(depth == TILE - 1, jnp.where(is_own, flag(mid[k], 5), z_hi_outer[side][k]), one))
            cross.append(jnp.where(crossing, flag(mid[k], d), one))
        x_lo = jnp.where(sub == 0, jnp.where(is_own, flag(own, 0), flag(col, 0)), one)
        x_hi = jnp.where(sub == 0, jnp.where(is_own, flag(own, 1), flag(col, 1)), one)
        x_gate = jnp.concatenate([one, x_lo, one, one, one, x_hi], axis=0)
        return x_gate, by_region(cross), by_region(z_lo), by_region(z_hi)

    lo_gates = strip_gates(0, col_lo, lane >= 64, lane // TILE == 2, 2)
    hi_gates = strip_gates(1, col_hi, lane < 32, lane // TILE == 1, 3)
    cross_lo = by_region([flag(tile, 2) for tile in mid])
    cross_hi = by_region([flag(tile, 3) for tile in mid])

    def strip(received, tiles, g):
        return jnp.concatenate([roll(tiles[0], 6 - 2 * g, 0), received[g], roll(tiles[1], -2 * g, 0)], axis=0)

    raw = [strip(recv_lo, corners[:2], g) for g in range(3)]
    outer = [roll(raw[0], 64, 1), raw[0], roll(raw[1], 64, 1), raw[1], roll(raw[2], 64, 1)]
    lo = [jnp.where(lane_long < 64, outer[f], roll(ext[f, :, 0, :], 64, 1)) for f in range(5)]
    raw = [strip(recv_hi, corners[2:], g) for g in range(3)]
    outer = [roll(raw[0], 32, 1), roll(raw[1], 32, 1), roll(raw[0], 96, 1), roll(raw[2], 32, 1), roll(raw[2], 96, 1)]
    hi = [jnp.where(lane_long < 32, roll(ext[f, :, 7, :], 32, 1), outer[f]) for f in range(5)]

    depth_long = lane_long % TILE

    def strip_below(v, gates):
        x_gate, y_gate, z_lo, _ = gates
        return (
            roll(v, 1, 0) * x_gate,
            roll(v, 32, 1) * y_gate,
            jnp.where(depth_long == 0, roll(v, -31, 1), roll(v, 1, 1)) * z_lo,
        )

    def strip_above(v, gates):
        x_gate, y_gate, _, z_hi = gates
        return (
            roll(v * x_gate, -1, 0),
            roll(v * y_gate, -32, 1),
            jnp.where(depth_long == TILE - 1, roll(v, 31, 1), roll(v, -1, 1)) * z_hi,
        )

    def strip_velocity(v, p, m, gates, wanted):
        under = strip_below(p, gates)
        result = []
        for d in wanted:
            b, a = strip_below(v[d], gates), strip_above(v[d], gates)
            laplace = (b[0] + a[0]) + (b[1] + a[1]) + (b[2] + a[2]) - 6.0 * v[d]
            result.append(v[d] + RATE * m * (force_ref[d] + laplace - (p - under[d])))
        return result

    def strip_pressure(v, p, m, gates):
        total = zero_strip
        for d in range(3):
            total = total + (strip_above(v[d], gates)[d] - v[d])
        return p + PRESSURE_RATE * (m * total)

    zero_strip = jnp.zeros((PLANES, 128), f32)

    def put_lo(dst, v):
        dst[:, 0, :] = roll(v, 64, 1) * cross_lo

    def put_hi(dst, v):
        dst[:, 7, :] = roll(v, 96, 1) * cross_hi

    lo1 = strip_velocity(lo[:3], lo[3], lo[4], lo_gates, (0, 1, 2))
    hi1 = strip_velocity(hi[:3], hi[3], hi[4], hi_gates, (0, 1, 2))
    for d in range(3):
        put_lo(halo1.at[d], lo1[d])
        put_hi(halo1.at[d], hi1[d])
    lo_p1 = strip_pressure(lo1, lo[3], lo[4], lo_gates)
    hi_p1 = strip_pressure(hi1, hi[3], hi[4], hi_gates)
    put_lo(halo1.at[3], lo_p1)

    for x, step in ((-1, 2), (31, 3)):
        sub3, lane3 = iotas((step, 8, 128))
        velocity_planes(x, step, ext, ext.at[3], None, vel1)
    scale_lo, scale_hi = RATE * ext[4, :, 0, :], RATE * ext[4, :, 7, :]
    for d in range(3):
        face = lo[d] + lo[3] if d == 1 else lo[d]
        vel1[d, :, 0, :] = vel1[d, :, 0, :] + jnp.where(lane_long < 32, scale_lo * (roll(face, 96, 1) * cross_lo), 0.0)
        vel1[d, :, 7, :] = vel1[d, :, 7, :] + jnp.where(lane_long >= 96, scale_hi * (roll(hi[d], 64, 1) * cross_hi), 0.0)

    hear(1)
    tell(2, 4)
    tell(3, 1)

    step = 5
    sub3, lane3 = iotas((step, 8, 128))
    for x in range(-1, 32, step):
        pres1[planes(x, step)] = ext[3, planes(x, step)] + PRESSURE_RATE * divergence_planes(x, step, vel1, halo1.at[1])

    hi1 = [jnp.where(lane_long < 32, roll(vel1[d, :, 7, :], 32, 1), hi1[d]) for d in range(3)]
    hi_p1 = jnp.where(lane_long < 32, roll(pres1[:, 7, :], 32, 1), hi_p1)
    put_hi(halo2, strip_velocity(hi1, hi_p1, hi[4], hi_gates, (1,))[0])

    step = 3
    sub3, lane3 = iotas((step, 8, 128))
    for x in range(0, 33, step):
        velocity_planes(x, step, vel1, pres1, halo1, vel2)

    step = 8
    sub3, lane3 = iotas((step, 8, 128))
    message = zero
    for x in range(0, TILE, step):
        div = divergence_planes(x, step, vel2, halo2)
        pres2[pl.ds(x, step)] = pres1[planes(x, step)] + PRESSURE_RATE * div
        part = jnp.sum(div, axis=0)
        for shift in (1, 2, 4):
            part = part + jnp.where((lane // shift) % 2 == 0, roll(part, -shift, 1), roll(part, shift, 1))
        part = part + roll(part, 32, 1)
        part = part + roll(part, 64, 1)
        part = part + jnp.where(sub % 2 == 0, roll(part, -1, 0), roll(part, 1, 0))
        message = jnp.where(jnp.logical_and(2 * (lane // 32) + (lane % 8) // 4 == x // 8, sub == 2 * (lane % 4)), part, message)
    table[0, z_count // 2] = jnp.sum(message, axis=0, keepdims=True)[:, :64] * (1.0 / 64.0)

    middle = z_count // 2

    def straight_copy(dy, at):
        return pltpu.make_async_remote_copy(
            src_ref=table.at[0, pl.ds(middle, 1)], dst_ref=straight.at[pl.ds(c, 1)], send_sem=dsend_sem.at[dy * MID + at], recv_sem=drecv_sem.at[0],
            device_id=(r, lax.rem(y + dy, y_count) * z_count + at), device_id_type=MESH)

    def straight_goes(dy, at):
        goes = z != at if dy == 0 else None
        if at == 0:
            awake = jnp.logical_or(r > 0, lax.rem(y + dy, y_count) > 0)
            goes = awake if goes is None else jnp.logical_and(goes, awake)
        return goes

    def for_each_straight(act):
        for dy in (2, 1, y_count - 1, 0):
            for at in range(MID if dy == 0 else DIRECT):
                goes = straight_goes(dy, at)
                if goes is None:
                    act(straight_copy(dy, at))
                else:
                    pl.when(goes)(functools.partial(act, straight_copy(dy, at)))

    for_each_straight(lambda copy: copy.start())

    hear(3)
    near = []
    for k in range(1, NEAR + 1):
        for sign in (1, -1):
            index = len(near)
            near.append(pltpu.make_async_remote_copy(
                src_ref=table.at[0, middle], dst_ref=table.at[0, middle - sign * k], send_sem=gsend_sem.at[index], recv_sem=grecv_sem.at[index],
                device_id=along(0, sign * k), device_id_type=MESH))
    for copy in reversed(near):
        copy.start()

    stores = []
    for s in range(8):
        lanes = pl.ds(128 * s, 128)
        stores.append(pltpu.make_async_copy(vel2.at[:, pl.ds(OFF, TILE), s], fields_out.at[pl.ds(0, 3), :, lanes], store_sem.at[s]))
        stores.append(pltpu.make_async_copy(pres2.at[:, s], fields_out.at[3, :, lanes], store_sem.at[8 + s]))
    for copy in stores:
        copy.start()

    hear(2)
    tell(4, 3)
    hear(5)

    for copy in near:
        copy.wait()
    hear(4)
    width = 2 * NEAR + 1
    block, below_block, above_block = pl.ds(middle - NEAR, width), pl.ds(0, width), pl.ds(2 * FAR, width)
    far = []
    for k, (sign, landed) in enumerate(((1, below_block), (-1, above_block))):
        far.append(pltpu.make_async_remote_copy(
            src_ref=table.at[0, block], dst_ref=table.at[0, landed], send_sem=gsend_sem.at[len(near) + k], recv_sem=grecv_sem.at[len(near) + k],
            device_id=along(0, sign * FAR), device_id_type=MESH))
    wanted = [lax.rem(z + sign * FAR + z_count, z_count) >= MID for sign in (1, -1)]
    for copy, needed in zip(far, wanted, strict=True):
        pl.when(needed)(copy.start)

    def y_copies(parts, first):
        result = []
        for j in range(1, y_count):
            for part in parts:
                index = first + len(result)
                result.append(pltpu.make_async_remote_copy(
                    src_ref=table.at[0, part], dst_ref=table.at[y_count - j, part], send_sem=gsend_sem.at[index], recv_sem=grecv_sem.at[index],
                    device_id=along(j, 0), device_id_type=MESH))
        return result

    across = y_copies([block], len(near) + 2)
    across_far = y_copies([below_block, above_block], len(near) + 2 + len(across))

    @pl.when(z >= MID)
    def _():
        for copy in across:
            copy.start()
        for copy in far:
            copy.wait_recv()
        for copy in across_far:
            copy.start()

    spot = lax.broadcasted_iota(jnp.int32, (64, 512), 1)
    entry = spot // 128 % 2 * 32 + spot % 4 * 8 + spot // 64 % 2 * 4 + spot // 8 % 4
    pick = jnp.where(lax.broadcasted_iota(jnp.int32, (64, 512), 0) == entry, 1.0, 0.0).astype(f32)
    spot = lax.broadcasted_iota(jnp.int32, (8, 512), 1)
    octant = spot // 256 * 4 + (spot // 32) % 2 * 2 + (spot // 4) % 2
    holds = lax.broadcasted_iota(jnp.int32, (8, 512), 0) == octant

    for copy, needed in zip(far, wanted, strict=True):
        pl.when(needed)(copy.wait_send)
    for_each_straight(lambda copy: copy.wait_send())

    sources = [source_ref[0, o] for o in range(8)]
    kept = [jnp.maximum(source, 0) for source in sources]

    def keep(o, taken):
        row_buf[pl.ds(o, 1), :] = jnp.where(sources[o] >= 0, taken, jnp.zeros_like(taken))

    def arrive(count):
        straight[pl.ds(c, 1)] = table[0, pl.ds(middle, 1)]
        arrived = straight.at[pl.ds(0, count)]
        pltpu.make_async_copy(arrived, arrived, drecv_sem.at[0]).wait()

    handed = pltpu.make_async_remote_copy(
        src_ref=straight, dst_ref=straight, send_sem=dsend_sem.at[y_count * MID], recv_sem=drecv_sem.at[1], device_id=(r, 0 * c), device_id_type=MESH)
    hands_on = jnp.logical_and(r == 0, c == cols - z_count + MID - 1)

    @pl.when(jnp.logical_and(is_direct, jnp.logical_not(is_late)))
    def _():
        arrive(cols - 1)

    @pl.when(is_mid)
    def _():
        arrive(z_count - 1)
        ring = straight.at[pl.ds(y * z_count, z_count)]
        shares = [
            pltpu.make_async_remote_copy(
                src_ref=ring, dst_ref=ring, send_sem=dsend_sem.at[y_count * MID + j], recv_sem=drecv_sem.at[1 + j], device_id=along(j, 0), device_id_type=MESH)
            for j in range(1, y_count)
        ]
        for copy in shares:
            copy.start()
        for copy in shares:
            copy.wait()

    pl.when(hands_on)(handed.start)
    pl.when(is_late)(handed.wait_recv)

    @pl.when(z < MID)
    def _():
        for o in range(8):
            keep(o, straight[kept[o]])

    @pl.when(z >= MID)
    def _():
        for copy in across + across_far:
            copy.wait()
        for o in range(8):
            dy = lax.rem(kept[o] // z_count - y + y_count, y_count)
            dz = lax.rem(lax.rem(kept[o], z_count) - z + z_count + middle, z_count)
            keep(o, table[dy, dz])

    spread = jnp.dot(row_buf[...], pick, preferred_element_type=f32, precision=lax.Precision.HIGHEST)
    coarse_out[...] = jnp.sum(jnp.where(holds, spread, 0.0), axis=0, keepdims=True)

    for copy in stores:
        copy.wait()
    pl.when(hands_on)(handed.wait_send)


def on_device(rows, fields, fluid_mask, body_force, neighbours, sources):
    y_count, z_count = 4, 32
    f32 = jnp.float32
    volume = lambda n: pltpu.VMEM((n, PLANES, 8, 128), f32)
    planes = lambda: pltpu.VMEM((PLANES, 8, 128), f32)
    any_space = pl.BlockSpec(memory_space=pl.ANY)
    hbm = pl.BlockSpec(memory_space=pltpu.HBM)
    new_fields, coarse = pl.pallas_call(
        functools.partial(kernel, rows, y_count, z_count),
        out_shape=(
            jax.ShapeDtypeStruct((4, TILE, TILE * TILE), f32),
            jax.ShapeDtypeStruct((1, 512), f32),
        ),
        in_specs=[hbm] * 5,
        out_specs=(any_space, pl.BlockSpec(memory_space=pltpu.VMEM)),
        scratch_shapes=[
            pltpu.SMEM((1, 6), jnp.int32),
            pltpu.SMEM((1, 8), jnp.int32),
            pltpu.SMEM((3,), f32),
            volume(6),
            pltpu.VMEM((TILE, 8, 128), jnp.int32),
            volume(3),
            planes(),
            volume(3),
            pltpu.VMEM((TILE, 8, 128), f32),
            volume(4),
            planes(),
            planes(),
            planes(),
            planes(),
            pltpu.VMEM((3, TILE, 128), f32),
            pltpu.VMEM((3, TILE, 128), f32),
            pltpu.VMEM((3, TILE, 128), f32),
            pltpu.VMEM((3, TILE, 128), f32),
            pltpu.VMEM((4, 8, 128), f32),
            pltpu.VMEM((4, 8, 128), f32),
            pltpu.VMEM((y_count, SLOTS, 1, 64), f32),
            pltpu.VMEM((y_count * z_count, 1, 64), f32),
            pltpu.VMEM((8, 64), f32),
            pltpu.SemaphoreType.DMA((19,)),
            pltpu.SemaphoreType.DMA((16,)),
            pltpu.SemaphoreType.DMA((8,)),
            pltpu.SemaphoreType.DMA((8,)),
            pltpu.SemaphoreType.DMA((GATHER_COPIES,)),
            pltpu.SemaphoreType.DMA((GATHER_COPIES,)),
            pltpu.SemaphoreType.DMA((y_count * MID + y_count,)),
            pltpu.SemaphoreType.DMA((1 + y_count,)),
            pltpu.SemaphoreType.REGULAR((6,)),
        ],
        compiler_params=pltpu.CompilerParams(
            collective_id=0, has_side_effects=True, vmem_limit_bytes=32 * 1024 * 1024
        ),
    )(
        *(
            pltpu.with_memory_space_constraint(array, pltpu.HBM)
            for array in (
                neighbours,
                sources,
                body_force,
                fields.reshape(4, TILE, TILE * TILE),
                fluid_mask.reshape(TILE, TILE * TILE),
            )
        )
    )
    return new_fields[None], coarse


def solution(mesh):
    return jax.shard_map(
        functools.partial(on_device, mesh.shape["row"]),
        mesh=mesh,
        in_specs=(
            P(("row", "col"), None, None, None),
            P(("row", "col"), None, None),
            P(),
            P(("row", "col"), None),
            P(("row", "col"), None),
        ),
        out_specs=(P(("row", "col"), None, None, None), P(("row", "col"), None)),
        check_vma=False,
    )
```

```python
import functools

import jax
import jax.numpy as jnp
from jax import lax
from jax.experimental import pallas as pl
from jax.experimental.pallas import tpu as pltpu
from jax.sharding import PartitionSpec as P

MESH = pl.DeviceIdType.MESH
TILE = 32
RATE = 0.8 / 6.0
PRESSURE_RATE = 0.5
OFF = 8
PLANES = 48
NEAR = 5
FAR = 11
SLOTS = 33
GATHER_COPIES = 2 * NEAR + 2 + 9
DIRECT = 4
MID = 7


def roll(values, shift, axis):
    return pltpu.roll(values, shift % values.shape[axis], axis)


def kernel(
    rows, y_count, z_count,
    neighbour_hbm, source_hbm, force_hbm, fields_ref, mask_ref, fields_out, coarse_out,
    neighbour_ref, source_ref, force_ref,
    ext, mask_raw, vel1, pres1, vel2, pres2, halo2, gate_x, gate_lo, gate_hi,
    send_lo, send_hi, recv_lo, recv_hi, send_corner, recv_corner, table, straight, row_buf,
    load_sem, store_sem, send_sem, recv_sem, gsend_sem, grecv_sem, dsend_sem, drecv_sem, know_sem,
):
    f32 = jnp.float32
    cols = y_count * z_count
    r = lax.axis_index("row")
    c = lax.axis_index("col")
    y, z = c // z_count, lax.rem(c, z_count)

    def tile_at(dr, dc):
        return (lax.rem(r + dr + rows, rows), lax.rem(c + dc + cols, cols))

    def along(dy, dz):
        return (r, lax.rem(y + dy, y_count) * z_count + lax.rem(z + dz + z_count, z_count))

    greeted = [tile_at(dr, dc) for dr in (-1, 1) for dc in (-1, 1)]
    greeted += [tile_at(0, -1), tile_at(0, 1), tile_at(-1, 0), tile_at(1, 0)]
    greeted += [along(0, -1), along(0, 1), along(1, 0), along(y_count - 1, 0)]
    barrier = pltpu.get_barrier_semaphore()
    for device in greeted:
        pl.semaphore_signal(barrier, inc=1, device_id=device, device_id_type=MESH)
    is_direct = z < DIRECT
    is_late = jnp.logical_and(r == 0, c == 0)

    @pl.when(jnp.logical_and(is_direct, jnp.logical_not(is_late)))
    def _():
        def greet(k, carry):
            pl.semaphore_signal(barrier, inc=1, device_id=(r, lax.rem(c + k, cols)), device_id_type=MESH)
            return carry

        lax.fori_loop(1, cols, greet, 0)

    is_mid = jnp.logical_and(z >= DIRECT, z < MID)

    @pl.when(is_mid)
    def _():
        def greet(k, carry):
            pl.semaphore_signal(barrier, inc=1, device_id=(r, y * z_count + lax.rem(z + k, z_count)), device_id_type=MESH)
            return carry

        lax.fori_loop(1, z_count, greet, 0)

    greetings = len(greeted) + y_count * DIRECT - jnp.where(jnp.logical_and(is_direct, jnp.logical_not(is_late)), 1, 0) - jnp.where(r == 0, 1, 0) + MID - DIRECT - jnp.where(is_mid, 1, 0)

    smalls = [
        pltpu.make_async_copy(neighbour_hbm, neighbour_ref, load_sem.at[16]),
        pltpu.make_async_copy(source_hbm, source_ref, load_sem.at[17]),
        pltpu.make_async_copy(force_hbm, force_ref, load_sem.at[18]),
    ]
    for copy in smalls:
        copy.start()

    loads = []
    for s in range(8):
        lanes = pl.ds(128 * s, 128)
        loads.append(pltpu.make_async_copy(fields_ref.at[:, :, lanes], ext.at[pl.ds(0, 4), pl.ds(OFF, TILE), s], load_sem.at[s]))
        loads.append(pltpu.make_async_copy(mask_ref.at[:, lanes], mask_raw.at[:, s], load_sem.at[8 + s]))
    for copy in loads:
        copy.start()

    sub = lax.broadcasted_iota(jnp.int32, (8, 128), 0)
    lane = lax.broadcasted_iota(jnp.int32, (8, 128), 1)
    depth = lane % TILE
    lane_long = lax.broadcasted_iota(jnp.int32, (PLANES, 128), 1)
    zero = jnp.zeros((8, 128), f32)
    one = jnp.ones((8, 128), f32)

    for copy in smalls:
        copy.wait()

    def link(direction, exists):
        return jnp.where(jnp.logical_and(neighbour_ref[0, direction] == 0, exists), 1.0, 0.0).astype(f32)

    links = [link(0, r > 0), link(1, r < rows - 1), link(2, c > 0), link(3, c < cols - 1), link(4, True), link(5, True)]
    own = zero
    for d in range(6):
        own = jnp.where(sub == d, links[d], own)

    for x in (0, 1, 2, 30, 31):
        ext[5, OFF + x] = own

    def flag(tile, d):
        return jnp.broadcast_to(tile[d : d + 1, :], (8, 128))

    own_z_lo = jnp.where(depth == 0, flag(own, 4), one)
    own_z_hi = jnp.where(depth == TILE - 1, flag(own, 5), one)
    gate_x[...] = jnp.ones((PLANES, 8, 128), f32)
    gate_x[OFF] = flag(own, 0)
    gate_x[OFF + TILE] = flag(own, 1)
    gate_lo[pl.ds(OFF, TILE)] = jnp.broadcast_to(own_z_lo[None], (TILE, 8, 128))
    gate_hi[pl.ds(OFF, TILE)] = jnp.broadcast_to(own_z_hi[None], (TILE, 8, 128))

    for copy in loads:
        copy.wait()
    ext[4, pl.ds(OFF, TILE)] = mask_raw[...].astype(f32)

    lane_tile = lax.broadcasted_iota(jnp.int32, (TILE, 128), 1)
    flags_tile = jnp.concatenate([own] * 4, axis=0)
    top = [ext[f, pl.ds(OFF, TILE), 7, :] for f in range(5)]
    send_hi[0] = jnp.where(lane_tile >= 64, top[0], roll(top[1], 64, 1))
    send_hi[1] = jnp.where(lane_tile >= 64, top[2], roll(top[3], 64, 1))
    send_hi[2] = jnp.where(lane_tile >= 64, top[4], flags_tile)
    low = [ext[f, pl.ds(OFF, TILE), 0, :] for f in range(5)]
    send_lo[0] = jnp.where(lane_tile < 64, low[0], roll(low[2], 64, 1))
    send_lo[1] = jnp.where(lane_tile < 96, low[1], flags_tile)
    send_lo[2] = jnp.where(lane_tile < 64, low[3], roll(low[4], 64, 1))

    def corner(packed, x, up):
        tile = jnp.where(sub == 6, flag(own, 4), flag(own, 5))
        for g in range(3):
            tile = jnp.where(sub // 2 == g, roll(packed[g, x : x + 8], 2 * g - up, 0), tile)
        return tile

    send_corner[0] = corner(send_hi, 24, 6)
    send_corner[1] = corner(send_hi, 0, 0)
    send_corner[2] = corner(send_lo, 24, 6)
    send_corner[3] = corner(send_lo, 0, 0)

    pl.semaphore_wait(barrier, greetings)

    plan = [(send_corner.at[k], recv_corner.at[k], offset) for k, offset in enumerate([(1, 1), (-1, 1), (1, -1), (-1, -1)])]
    plan += [(send_hi, recv_lo, (0, 1)), (send_lo, recv_hi, (0, -1))]
    faces = []
    for k, (src, dst, offset) in enumerate(plan):
        faces.append(pltpu.make_async_remote_copy(
            src_ref=src, dst_ref=dst, send_sem=send_sem.at[k], recv_sem=recv_sem.at[k], device_id=tile_at(*offset), device_id_type=MESH))
    faces.append(pltpu.make_async_remote_copy(
        src_ref=ext.at[:, pl.ds(OFF + 30, 2)], dst_ref=ext.at[:, pl.ds(OFF - 2, 2)], send_sem=send_sem.at[6], recv_sem=recv_sem.at[6],
        device_id=tile_at(1, 0), device_id_type=MESH))
    faces.append(pltpu.make_async_remote_copy(
        src_ref=ext.at[:, pl.ds(OFF, 3)], dst_ref=ext.at[:, pl.ds(OFF + TILE, 3)], send_sem=send_sem.at[7], recv_sem=recv_sem.at[7],
        device_id=tile_at(-1, 0), device_id_type=MESH))
    for copy in faces:
        copy.start()

    def tell(step, reach):
        for device in (along(0, reach), along(0, -reach)):
            pl.semaphore_signal(know_sem.at[step], inc=1, device_id=device, device_id_type=MESH)

    def hear(step):
        pl.semaphore_wait(know_sem.at[step], 2)

    tell(0, 1)
    for j in (1, y_count - 1):
        pl.semaphore_signal(know_sem.at[5], inc=1, device_id=along(j, 0), device_id_type=MESH)

    def iotas(shape):
        return lax.broadcasted_iota(jnp.int32, shape, 1), lax.broadcasted_iota(jnp.int32, shape, 2)

    def below_y(v, h):
        w = jnp.where(sub3 == 0, 0.0 if h is None else h, roll(v, 1, 1))
        return roll(jnp.where(lane3 >= 96, w, v), 32, 2)

    def above_y(v, h):
        w = jnp.where(sub3 == 7, 0.0 if h is None else h, roll(v, -1, 1))
        return roll(jnp.where(lane3 < 32, w, v), -32, 2)

    def below_z(v, g):
        return jnp.where(lane3 % TILE == 0, roll(v, -31, 2), roll(v, 1, 2)) * g

    def above_z(v, g):
        return jnp.where(lane3 % TILE == TILE - 1, roll(v, 31, 2), roll(v, -1, 2)) * g

    def planes(x, n):
        return pl.ds(OFF + x, n)

    def velocity_planes(x, n, v_in, p_in, halo, v_out):
        here, under, over = planes(x, n), planes(x - 1, n), planes(x + 1, n)
        g_under, g_over, g_lo, g_hi = gate_x[here], gate_x[over], gate_lo[here], gate_hi[here]
        scale = RATE * ext[4, here]
        p = p_in[here]
        p_below = (p_in[under] * g_under, below_y(p, None if halo is None else halo[3, here]), below_z(p, g_lo))
        for d in range(3):
            v, h = v_in[d, here], None if halo is None else halo[d, here]
            total = (v_in[d, under] * g_under + v_in[d, over] * g_over) + (below_y(v, h) + above_y(v, h))
            total = total + (below_z(v, g_lo) + above_z(v, g_hi)) - 6.0 * v
            v_out[d, here] = v + scale * (force_ref[d] + total - (p - p_below[d]))

    def divergence_planes(x, n, v_in, halo_y):
        here, over = planes(x, n), planes(x + 1, n)
        vx, vy, vz = v_in[0, here], v_in[1, here], v_in[2, here]
        total = (v_in[0, over] * gate_x[over] - vx) + (above_y(vy, None if halo_y is None else halo_y[here]) - vy) + (above_z(vz, gate_hi[here]) - vz)
        return ext[4, here] * total

    step, shape3 = 5, (5, 8, 128)
    sub3, lane3 = iotas(shape3)
    for x in range(1, 31, step):
        velocity_planes(x, step, ext, ext.at[3], None, vel1)
        if x == 1:
            hear(0)
            tell(1, 2)
    for x, step in ((1, 5), (6, 5), (11, 5), (16, 5), (21, 5), (26, 4)):
        sub3, lane3 = iotas((step, 8, 128))
        pres1[planes(x, step)] = ext[3, planes(x, step)] + PRESSURE_RATE * divergence_planes(x, step, vel1, None)
    step = 4
    sub3, lane3 = iotas((step, 8, 128))
    for x in range(2, 30, step):
        velocity_planes(x, step, vel1, pres1, None, vel2)

    for copy in faces:
        copy.wait()

    row_lo, row_hi = ext[5, OFF - 1], ext[5, OFF + TILE]

    def spread_lo(tile):
        return jnp.where(lane < 64, tile, roll(tile, 64, 1))

    def spread_hi(tile):
        half = jnp.where(lane >= 96, tile, roll(tile, 96, 1))
        return jnp.where(lane >= 64, half, roll(half, 64, 1))

    corners = [recv_corner[k] for k in range(4)]
    col_lo, col_hi = spread_lo(recv_lo[2, 0:8]), spread_hi(recv_hi[1, 0:8])
    z_lo_outer = [(flag(corners[k], 6), flag(col, 4), flag(corners[k + 1], 6)) for k, col in ((0, col_lo), (2, col_hi))]
    z_hi_outer = [(flag(corners[k], 7), flag(col, 5), flag(corners[k + 1], 7)) for k, col in ((0, col_lo), (2, col_hi))]
    mid = [row_lo, own, row_hi]
    for k, x, n in ((0, OFF - 2, 2), (2, OFF + TILE, 3)):
        gate_lo[pl.ds(x, n)] = jnp.broadcast_to(jnp.where(depth == 0, flag(mid[k], 4), one)[None], (n, 8, 128))
        gate_hi[pl.ds(x, n)] = jnp.broadcast_to(jnp.where(depth == TILE - 1, flag(mid[k], 5), one)[None], (n, 8, 128))

    def by_region(tiles):
        return jnp.concatenate([tiles[0]] + [tiles[1]] * 4 + [tiles[2]], axis=0)

    def strip_gates(side, col, is_own, crossing, d):
        z_lo, z_hi, cross = [], [], []
        for k in range(3):
            z_lo.append(jnp.where(depth == 0, jnp.where(is_own, flag(mid[k], 4), z_lo_outer[side][k]), one))
            z_hi.append(jnp.where(depth == TILE - 1, jnp.where(is_own, flag(mid[k], 5), z_hi_outer[side][k]), one))
            cross.append(jnp.where(crossing, flag(mid[k], d), one))
        x_lo = jnp.where(sub == 0, jnp.where(is_own, flag(own, 0), flag(col, 0)), one)
        x_hi = jnp.where(sub == 0, jnp.where(is_own, flag(own, 1), flag(col, 1)), one)
        x_gate = jnp.concatenate([one, x_lo, one, one, one, x_hi], axis=0)
        return x_gate, by_region(cross), by_region(z_lo), by_region(z_hi)

    lo_gates = strip_gates(0, col_lo, lane >= 64, lane // TILE == 2, 2)
    hi_gates = strip_gates(1, col_hi, lane < 32, lane // TILE == 1, 3)
    cross_lo = by_region([flag(tile, 2) for tile in mid])
    cross_hi = by_region([flag(tile, 3) for tile in mid])

    def strip(received, tiles, g):
        return jnp.concatenate([roll(tiles[0], 6 - 2 * g, 0), received[g], roll(tiles[1], -2 * g, 0)], axis=0)

    raw = [strip(recv_lo, corners[:2], g) for g in range(3)]
    outer = [roll(raw[0], 64, 1), raw[0], roll(raw[1], 64, 1), raw[1], roll(raw[2], 64, 1)]
    lo = [jnp.where(lane_long < 64, outer[f], roll(ext[f, :, 0, :], 64, 1)) for f in range(5)]
    raw = [strip(recv_hi, corners[2:], g) for g in range(3)]
    outer = [roll(raw[0], 32, 1), roll(raw[1], 32, 1), roll(raw[0], 96, 1), roll(raw[2], 32, 1), roll(raw[2], 96, 1)]
    hi = [jnp.where(lane_long < 32, roll(ext[f, :, 7, :], 32, 1), outer[f]) for f in range(5)]

    depth_long = lane_long % TILE

    def strip_below(v, gates):
        x_gate, y_gate, z_lo, _ = gates
        return (
            roll(v, 1, 0) * x_gate,
            roll(v, 32, 1) * y_gate,
            jnp.where(depth_long == 0, roll(v, -31, 1), roll(v, 1, 1)) * z_lo,
        )

    def strip_above(v, gates):
        x_gate, y_gate, _, z_hi = gates
        return (
            roll(v * x_gate, -1, 0),
            roll(v * y_gate, -32, 1),
            jnp.where(depth_long == TILE - 1, roll(v, 31, 1), roll(v, -1, 1)) * z_hi,
        )

    def strip_velocity(v, p, m, gates, wanted):
        under = strip_below(p, gates)
        result = []
        for d in wanted:
            b, a = strip_below(v[d], gates), strip_above(v[d], gates)
            laplace = (b[0] + a[0]) + (b[1] + a[1]) + (b[2] + a[2]) - 6.0 * v[d]
            result.append(v[d] + RATE * m * (force_ref[d] + laplace - (p - under[d])))
        return result

    def strip_pressure(v, p, m, gates):
        total = zero_strip
        for d in range(3):
            total = total + (strip_above(v[d], gates)[d] - v[d])
        return p + PRESSURE_RATE * (m * total)

    zero_strip = jnp.zeros((PLANES, 128), f32)

    def put_hi(dst, v):
        dst[:, 7, :] = roll(v, 96, 1) * cross_hi

    lo1 = strip_velocity(lo[:3], lo[3], lo[4], lo_gates, (0, 1, 2))
    hi1 = strip_velocity(hi[:3], hi[3], hi[4], hi_gates, (0, 1, 2))
    lo_p1 = strip_pressure(lo1, lo[3], lo[4], lo_gates)
    hi_p1 = strip_pressure(hi1, hi[3], hi[4], hi_gates)

    for x, step in ((-1, 2), (31, 3)):
        sub3, lane3 = iotas((step, 8, 128))
        velocity_planes(x, step, ext, ext.at[3], None, vel1)
    scale_lo, scale_hi = RATE * ext[4, :, 0, :], RATE * ext[4, :, 7, :]
    for d in range(3):
        face = lo[d] + lo[3] if d == 1 else lo[d]
        vel1[d, :, 0, :] = vel1[d, :, 0, :] + jnp.where(lane_long < 32, scale_lo * (roll(face, 96, 1) * cross_lo), 0.0)
        vel1[d, :, 7, :] = vel1[d, :, 7, :] + jnp.where(lane_long >= 96, scale_hi * (roll(hi[d], 64, 1) * cross_hi), 0.0)

    hear(1)
    tell(2, 4)
    tell(3, 1)

    for x, step in ((-1, 2), (30, 3)):
        sub3, lane3 = iotas((step, 8, 128))
        pres1[planes(x, step)] = ext[3, planes(x, step)] + PRESSURE_RATE * divergence_planes(x, step, vel1, None)

    x_own = jnp.concatenate([one, jnp.where(sub == 0, flag(own, 0), one), one, one, one, jnp.where(sub == 0, flag(own, 1), one)], axis=0)
    z_lo_own = by_region([jnp.where(depth == 0, flag(tile, 4), one) for tile in mid])
    z_hi_own = by_region([jnp.where(depth == TILE - 1, flag(tile, 5), one) for tile in mid])

    def edge_below(v, under_y):
        return (
            roll(v, 1, 0) * x_own,
            jnp.where(lane_long < 32, under_y, roll(v, 32, 1)),
            jnp.where(depth_long == 0, roll(v, -31, 1), roll(v, 1, 1)) * z_lo_own,
        )

    def edge_above(v, over_y):
        return (
            roll(v * x_own, -1, 0),
            jnp.where(lane_long >= 96, over_y, roll(v, -32, 1)),
            jnp.where(depth_long == TILE - 1, roll(v, 31, 1), roll(v, -1, 1)) * z_hi_own,
        )

    def over_edge(ref, strip_values, s):
        return roll(ref[:, 1, :], 96, 1) if s == 0 else roll(strip_values, 64, 1) * cross_hi

    def under_edge(ref, strip_values, s):
        return roll(strip_values, 96, 1) * cross_lo if s == 0 else roll(ref[:, 6, :], 32, 1)

    for s in (0, 7):
        total = zero_strip
        for d in range(3):
            v = vel1[d, :, s, :]
            total = total + (edge_above(v, over_edge(vel1.at[d], hi1[d], s))[d] - v)
        pres1[:, s, :] = ext[3, :, s, :] + PRESSURE_RATE * (ext[4, :, s, :] * total)

    hi1_full = [jnp.where(lane_long < 32, roll(vel1[d, :, 7, :], 32, 1), hi1[d]) for d in range(3)]
    hi_p1 = jnp.where(lane_long < 32, roll(pres1[:, 7, :], 32, 1), hi_p1)
    put_hi(halo2, strip_velocity(hi1_full, hi_p1, hi[4], hi_gates, (1,))[0])

    for x, step in ((0, 2), (30, 3)):
        sub3, lane3 = iotas((step, 8, 128))
        velocity_planes(x, step, vel1, pres1, None, vel2)
    for s in (0, 7):
        p, scale = pres1[:, s, :], RATE * ext[4, :, s, :]
        p_below = edge_below(p, under_edge(pres1, lo_p1, s))
        for d in range(3):
            v = vel1[d, :, s, :]
            b = edge_below(v, under_edge(vel1.at[d], lo1[d], s))
            a = edge_above(v, over_edge(vel1.at[d], hi1[d], s))
            laplace = (b[0] + a[0]) + (b[1] + a[1]) + (b[2] + a[2]) - 6.0 * v
            vel2[d, :, s, :] = v + scale * (force_ref[d] + laplace - (p - p_below[d]))

    step = 8
    sub3, lane3 = iotas((step, 8, 128))
    message = zero
    for x in range(0, TILE, step):
        div = divergence_planes(x, step, vel2, halo2)
        pres2[pl.ds(x, step)] = pres1[planes(x, step)] + PRESSURE_RATE * div
        part = jnp.sum(div, axis=0)
        for shift in (1, 2, 4):
            part = part + jnp.where((lane // shift) % 2 == 0, roll(part, -shift, 1), roll(part, shift, 1))
        part = part + roll(part, 32, 1)
        part = part + roll(part, 64, 1)
        part = part + jnp.where(sub % 2 == 0, roll(part, -1, 0), roll(part, 1, 0))
        message = jnp.where(jnp.logical_and(2 * (lane // 32) + (lane % 8) // 4 == x // 8, sub == 2 * (lane % 4)), part, message)
    table[0, z_count // 2] = jnp.sum(message, axis=0, keepdims=True)[:, :64] * (1.0 / 64.0)

    middle = z_count // 2

    def straight_copy(dy, at):
        return pltpu.make_async_remote_copy(
            src_ref=table.at[0, pl.ds(middle, 1)], dst_ref=straight.at[pl.ds(c, 1)], send_sem=dsend_sem.at[dy * MID + at], recv_sem=drecv_sem.at[0],
            device_id=(r, lax.rem(y + dy, y_count) * z_count + at), device_id_type=MESH)

    def straight_goes(dy, at):
        goes = z != at if dy == 0 else None
        if at == 0:
            awake = jnp.logical_or(r > 0, lax.rem(y + dy, y_count) > 0)
            goes = awake if goes is None else jnp.logical_and(goes, awake)
        return goes

    def for_each_straight(act):
        for dy in (2, 1, y_count - 1, 0):
            for at in range(MID if dy == 0 else DIRECT):
                goes = straight_goes(dy, at)
                if goes is None:
                    act(straight_copy(dy, at))
                else:
                    pl.when(goes)(functools.partial(act, straight_copy(dy, at)))

    for_each_straight(lambda copy: copy.start())

    hear(3)
    near = []
    for k in range(1, NEAR + 1):
        for sign in (1, -1):
            index = len(near)
            near.append(pltpu.make_async_remote_copy(
                src_ref=table.at[0, middle], dst_ref=table.at[0, middle - sign * k], send_sem=gsend_sem.at[index], recv_sem=grecv_sem.at[index],
                device_id=along(0, sign * k), device_id_type=MESH))
    for copy in reversed(near):
        copy.start()

    stores = []
    for s in range(8):
        lanes = pl.ds(128 * s, 128)
        stores.append(pltpu.make_async_copy(vel2.at[:, pl.ds(OFF, TILE), s], fields_out.at[pl.ds(0, 3), :, lanes], store_sem.at[s]))
        stores.append(pltpu.make_async_copy(pres2.at[:, s], fields_out.at[3, :, lanes], store_sem.at[8 + s]))
    for copy in stores:
        copy.start()

    hear(2)
    tell(4, 3)
    hear(5)

    for copy in near:
        copy.wait()
    hear(4)
    width = 2 * NEAR + 1
    block, below_block, above_block = pl.ds(middle - NEAR, width), pl.ds(0, width), pl.ds(2 * FAR, width)
    far = []
    for k, (sign, landed) in enumerate(((1, below_block), (-1, above_block))):
        far.append(pltpu.make_async_remote_copy(
            src_ref=table.at[0, block], dst_ref=table.at[0, landed], send_sem=gsend_sem.at[len(near) + k], recv_sem=grecv_sem.at[len(near) + k],
            device_id=along(0, sign * FAR), device_id_type=MESH))
    wanted = [lax.rem(z + sign * FAR + z_count, z_count) >= MID for sign in (1, -1)]
    for copy, needed in zip(far, wanted, strict=True):
        pl.when(needed)(copy.start)

    def y_copies(parts, first):
        result = []
        for j in range(1, y_count):
            for part in parts:
                index = first + len(result)
                result.append(pltpu.make_async_remote_copy(
                    src_ref=table.at[0, part], dst_ref=table.at[y_count - j, part], send_sem=gsend_sem.at[index], recv_sem=grecv_sem.at[index],
                    device_id=along(j, 0), device_id_type=MESH))
        return result

    across = y_copies([block], len(near) + 2)
    across_far = y_copies([below_block, above_block], len(near) + 2 + len(across))

    @pl.when(z >= MID)
    def _():
        for copy in across:
            copy.start()
        for copy in far:
            copy.wait_recv()
        for copy in across_far:
            copy.start()

    spot = lax.broadcasted_iota(jnp.int32, (64, 512), 1)
    entry = spot // 128 % 2 * 32 + spot % 4 * 8 + spot // 64 % 2 * 4 + spot // 8 % 4
    pick = jnp.where(lax.broadcasted_iota(jnp.int32, (64, 512), 0) == entry, 1.0, 0.0).astype(f32)
    spot = lax.broadcasted_iota(jnp.int32, (8, 512), 1)
    octant = spot // 256 * 4 + (spot // 32) % 2 * 2 + (spot // 4) % 2
    holds = lax.broadcasted_iota(jnp.int32, (8, 512), 0) == octant

    for copy, needed in zip(far, wanted, strict=True):
        pl.when(needed)(copy.wait_send)
    for_each_straight(lambda copy: copy.wait_send())

    sources = [source_ref[0, o] for o in range(8)]
    kept = [jnp.maximum(source, 0) for source in sources]

    def keep(o, taken):
        row_buf[pl.ds(o, 1), :] = jnp.where(sources[o] >= 0, taken, jnp.zeros_like(taken))

    def arrive(count):
        straight[pl.ds(c, 1)] = table[0, pl.ds(middle, 1)]
        arrived = straight.at[pl.ds(0, count)]
        pltpu.make_async_copy(arrived, arrived, drecv_sem.at[0]).wait()

    handed = pltpu.make_async_remote_copy(
        src_ref=straight, dst_ref=straight, send_sem=dsend_sem.at[y_count * MID], recv_sem=drecv_sem.at[1], device_id=(r, 0 * c), device_id_type=MESH)
    hands_on = jnp.logical_and(r == 0, c == cols - z_count + MID - 1)

    @pl.when(jnp.logical_and(is_direct, jnp.logical_not(is_late)))
    def _():
        arrive(cols - 1)

    @pl.when(is_mid)
    def _():
        arrive(z_count - 1)
        ring = straight.at[pl.ds(y * z_count, z_count)]
        shares = [
            pltpu.make_async_remote_copy(
                src_ref=ring, dst_ref=ring, send_sem=dsend_sem.at[y_count * MID + j], recv_sem=drecv_sem.at[1 + j], device_id=along(j, 0), device_id_type=MESH)
            for j in range(1, y_count)
        ]
        for copy in shares:
            copy.start()
        for copy in shares:
            copy.wait()

    pl.when(hands_on)(handed.start)
    pl.when(is_late)(handed.wait_recv)

    @pl.when(z < MID)
    def _():
        for o in range(8):
            keep(o, straight[kept[o]])

    @pl.when(z >= MID)
    def _():
        for copy in across + across_far:
            copy.wait()
        for o in range(8):
            dy = lax.rem(kept[o] // z_count - y + y_count, y_count)
            dz = lax.rem(lax.rem(kept[o], z_count) - z + z_count + middle, z_count)
            keep(o, table[dy, dz])

    spread = jnp.dot(row_buf[...], pick, preferred_element_type=f32, precision=lax.Precision.HIGHEST)
    coarse_out[...] = jnp.sum(jnp.where(holds, spread, 0.0), axis=0, keepdims=True)

    for copy in stores:
        copy.wait()
    pl.when(hands_on)(handed.wait_send)


def on_device(rows, fields, fluid_mask, body_force, neighbours, sources):
    y_count, z_count = 4, 32
    f32 = jnp.float32
    volume = lambda n: pltpu.VMEM((n, PLANES, 8, 128), f32)
    planes = lambda: pltpu.VMEM((PLANES, 8, 128), f32)
    any_space = pl.BlockSpec(memory_space=pl.ANY)
    hbm = pl.BlockSpec(memory_space=pltpu.HBM)
    new_fields, coarse = pl.pallas_call(
        functools.partial(kernel, rows, y_count, z_count),
        out_shape=(
            jax.ShapeDtypeStruct((4, TILE, TILE * TILE), f32),
            jax.ShapeDtypeStruct((1, 512), f32),
        ),
        in_specs=[hbm] * 5,
        out_specs=(any_space, pl.BlockSpec(memory_space=pltpu.VMEM)),
        scratch_shapes=[
            pltpu.SMEM((1, 6), jnp.int32),
            pltpu.SMEM((1, 8), jnp.int32),
            pltpu.SMEM((3,), f32),
            volume(6),
            pltpu.VMEM((TILE, 8, 128), jnp.int32),
            volume(3),
            planes(),
            volume(3),
            pltpu.VMEM((TILE, 8, 128), f32),
            planes(),
            planes(),
            planes(),
            planes(),
            pltpu.VMEM((3, TILE, 128), f32),
            pltpu.VMEM((3, TILE, 128), f32),
            pltpu.VMEM((3, TILE, 128), f32),
            pltpu.VMEM((3, TILE, 128), f32),
            pltpu.VMEM((4, 8, 128), f32),
            pltpu.VMEM((4, 8, 128), f32),
            pltpu.VMEM((y_count, SLOTS, 1, 64), f32),
            pltpu.VMEM((y_count * z_count, 1, 64), f32),
            pltpu.VMEM((8, 64), f32),
            pltpu.SemaphoreType.DMA((19,)),
            pltpu.SemaphoreType.DMA((16,)),
            pltpu.SemaphoreType.DMA((8,)),
            pltpu.SemaphoreType.DMA((8,)),
            pltpu.SemaphoreType.DMA((GATHER_COPIES,)),
            pltpu.SemaphoreType.DMA((GATHER_COPIES,)),
            pltpu.SemaphoreType.DMA((y_count * MID + y_count,)),
            pltpu.SemaphoreType.DMA((1 + y_count,)),
            pltpu.SemaphoreType.REGULAR((6,)),
        ],
        compiler_params=pltpu.CompilerParams(
            collective_id=0, has_side_effects=True, vmem_limit_bytes=32 * 1024 * 1024
        ),
    )(
        *(
            pltpu.with_memory_space_constraint(array, pltpu.HBM)
            for array in (
                neighbours,
                sources,
                body_force,
                fields.reshape(4, TILE, TILE * TILE),
                fluid_mask.reshape(TILE, TILE * TILE),
            )
        )
    )
    return new_fields[None], coarse


def solution(mesh):
    return jax.shard_map(
        functools.partial(on_device, mesh.shape["row"]),
        mesh=mesh,
        in_specs=(
            P(("row", "col"), None, None, None),
            P(("row", "col"), None, None),
            P(),
            P(("row", "col"), None),
            P(("row", "col"), None),
        ),
        out_specs=(P(("row", "col"), None, None, None), P(("row", "col"), None)),
        check_vma=False,
    )
```

```python
import functools

import jax
import jax.numpy as jnp
from jax import lax
from jax.experimental import pallas as pl
from jax.experimental.pallas import tpu as pltpu
from jax.sharding import PartitionSpec as P

MESH = pl.DeviceIdType.MESH
TILE = 32
RATE = 0.8 / 6.0
PRESSURE_RATE = 0.5
OFF = 8
PLANES = 48
NEAR = 5
FAR = 11
SLOTS = 33
GATHER_COPIES = 2 * NEAR + 2 + 9
DIRECT = 4
MID = 7


def roll(values, shift, axis):
    return pltpu.roll(values, shift % values.shape[axis], axis)


def kernel(
    rows, y_count, z_count,
    neighbour_hbm, source_hbm, force_hbm, fields_ref, mask_ref, fields_out, coarse_out,
    neighbour_ref, source_ref, force_ref,
    ext, mask_raw, vel1, pres1, vel2, pres2, halo2, gate_x, gate_lo, gate_hi,
    send_lo, send_hi, recv_lo, recv_hi, send_corner, recv_corner, table, straight, row_buf,
    load_sem, store_sem, send_sem, recv_sem, gsend_sem, grecv_sem, dsend_sem, drecv_sem, know_sem,
):
    f32 = jnp.float32
    cols = y_count * z_count
    r = lax.axis_index("row")
    c = lax.axis_index("col")
    y, z = c // z_count, lax.rem(c, z_count)

    def tile_at(dr, dc):
        return (lax.rem(r + dr + rows, rows), lax.rem(c + dc + cols, cols))

    def along(dy, dz):
        return (r, lax.rem(y + dy, y_count) * z_count + lax.rem(z + dz + z_count, z_count))

    greeted = [tile_at(dr, dc) for dr in (-1, 1) for dc in (-1, 1)]
    greeted += [tile_at(0, -1), tile_at(0, 1), tile_at(-1, 0), tile_at(1, 0)]
    greeted += [along(0, -1), along(0, 1), along(1, 0), along(y_count - 1, 0)]
    barrier = pltpu.get_barrier_semaphore()
    for device in greeted:
        pl.semaphore_signal(barrier, inc=1, device_id=device, device_id_type=MESH)
    is_direct = z < DIRECT
    is_late = jnp.logical_and(r == 0, c == 0)

    @pl.when(jnp.logical_and(is_direct, jnp.logical_not(is_late)))
    def _():
        def greet(k, carry):
            pl.semaphore_signal(barrier, inc=1, device_id=(r, lax.rem(c + k, cols)), device_id_type=MESH)
            return carry

        lax.fori_loop(1, cols, greet, 0)

    is_mid = jnp.logical_and(z >= DIRECT, z < MID)

    @pl.when(is_mid)
    def _():
        def greet(k, carry):
            pl.semaphore_signal(barrier, inc=1, device_id=(r, y * z_count + lax.rem(z + k, z_count)), device_id_type=MESH)
            return carry

        lax.fori_loop(1, z_count, greet, 0)

    greetings = len(greeted) + y_count * DIRECT - jnp.where(jnp.logical_and(is_direct, jnp.logical_not(is_late)), 1, 0) - jnp.where(r == 0, 1, 0) + MID - DIRECT - jnp.where(is_mid, 1, 0)

    smalls = [
        pltpu.make_async_copy(neighbour_hbm, neighbour_ref, load_sem.at[16]),
        pltpu.make_async_copy(source_hbm, source_ref, load_sem.at[17]),
        pltpu.make_async_copy(force_hbm, force_ref, load_sem.at[18]),
    ]
    for copy in smalls:
        copy.start()

    loads = []
    for s in range(8):
        lanes = pl.ds(128 * s, 128)
        loads.append(pltpu.make_async_copy(fields_ref.at[:, :, lanes], ext.at[pl.ds(0, 4), pl.ds(OFF, TILE), s], load_sem.at[s]))
        loads.append(pltpu.make_async_copy(mask_ref.at[:, lanes], mask_raw.at[:, s], load_sem.at[8 + s]))
    for copy in loads:
        copy.start()

    sub = lax.broadcasted_iota(jnp.int32, (8, 128), 0)
    lane = lax.broadcasted_iota(jnp.int32, (8, 128), 1)
    depth = lane % TILE
    lane_long = lax.broadcasted_iota(jnp.int32, (PLANES, 128), 1)
    zero = jnp.zeros((8, 128), f32)
    one = jnp.ones((8, 128), f32)

    for copy in smalls:
        copy.wait()

    def link(direction, exists):
        return jnp.where(jnp.logical_and(neighbour_ref[0, direction] == 0, exists), 1.0, 0.0).astype(f32)

    links = [link(0, r > 0), link(1, r < rows - 1), link(2, c > 0), link(3, c < cols - 1), link(4, True), link(5, True)]
    own = zero
    for d in range(6):
        own = jnp.where(sub == d, links[d], own)

    for x in (0, 1, 2, 30, 31):
        ext[5, OFF + x] = own

    def flag(tile, d):
        return jnp.broadcast_to(tile[d : d + 1, :], (8, 128))

    own_z_lo = jnp.where(depth == 0, flag(own, 4), one)
    own_z_hi = jnp.where(depth == TILE - 1, flag(own, 5), one)
    gate_x[...] = jnp.ones((PLANES, 8, 128), f32)
    gate_x[OFF] = flag(own, 0)
    gate_x[OFF + TILE] = flag(own, 1)
    gate_lo[pl.ds(OFF, TILE)] = jnp.broadcast_to(own_z_lo[None], (TILE, 8, 128))
    gate_hi[pl.ds(OFF, TILE)] = jnp.broadcast_to(own_z_hi[None], (TILE, 8, 128))

    for copy in loads:
        copy.wait()
    ext[4, pl.ds(OFF, TILE)] = mask_raw[...].astype(f32)

    lane_tile = lax.broadcasted_iota(jnp.int32, (TILE, 128), 1)
    flags_tile = jnp.concatenate([own] * 4, axis=0)
    top = [ext[f, pl.ds(OFF, TILE), 7, :] for f in range(5)]
    send_hi[0] = jnp.where(lane_tile >= 64, top[0], roll(top[1], 64, 1))
    send_hi[1] = jnp.where(lane_tile >= 64, top[2], roll(top[3], 64, 1))
    send_hi[2] = jnp.where(lane_tile >= 64, top[4], flags_tile)
    low = [ext[f, pl.ds(OFF, TILE), 0, :] for f in range(5)]
    send_lo[0] = jnp.where(lane_tile < 64, low[0], roll(low[2], 64, 1))
    send_lo[1] = jnp.where(lane_tile < 96, low[1], flags_tile)
    send_lo[2] = jnp.where(lane_tile < 64, low[3], roll(low[4], 64, 1))

    def corner(packed, x, up):
        tile = jnp.where(sub == 6, flag(own, 4), flag(own, 5))
        for g in range(3):
            tile = jnp.where(sub // 2 == g, roll(packed[g, x : x + 8], 2 * g - up, 0), tile)
        return tile

    send_corner[0] = corner(send_hi, 24, 6)
    send_corner[1] = corner(send_hi, 0, 0)
    send_corner[2] = corner(send_lo, 24, 6)
    send_corner[3] = corner(send_lo, 0, 0)

    pl.semaphore_wait(barrier, greetings)

    plan = [(send_corner.at[k], recv_corner.at[k], offset) for k, offset in enumerate([(1, 1), (-1, 1), (1, -1), (-1, -1)])]
    plan += [(send_hi, recv_lo, (0, 1)), (send_lo, recv_hi, (0, -1))]
    faces = []
    for k, (src, dst, offset) in enumerate(plan):
        faces.append(pltpu.make_async_remote_copy(
            src_ref=src, dst_ref=dst, send_sem=send_sem.at[k], recv_sem=recv_sem.at[k], device_id=tile_at(*offset), device_id_type=MESH))
    faces.append(pltpu.make_async_remote_copy(
        src_ref=ext.at[:, pl.ds(OFF + 30, 2)], dst_ref=ext.at[:, pl.ds(OFF - 2, 2)], send_sem=send_sem.at[6], recv_sem=recv_sem.at[6],
        device_id=tile_at(1, 0), device_id_type=MESH))
    faces.append(pltpu.make_async_remote_copy(
        src_ref=ext.at[:, pl.ds(OFF, 3)], dst_ref=ext.at[:, pl.ds(OFF + TILE, 3)], send_sem=send_sem.at[7], recv_sem=recv_sem.at[7],
        device_id=tile_at(-1, 0), device_id_type=MESH))
    for copy in faces:
        copy.start()

    def tell(step, reach):
        for device in (along(0, reach), along(0, -reach)):
            pl.semaphore_signal(know_sem.at[step], inc=1, device_id=device, device_id_type=MESH)

    def hear(step):
        pl.semaphore_wait(know_sem.at[step], 2)

    tell(0, 1)
    for j in (1, y_count - 1):
        pl.semaphore_signal(know_sem.at[5], inc=1, device_id=along(j, 0), device_id_type=MESH)

    def iotas(shape):
        return lax.broadcasted_iota(jnp.int32, shape, 1), lax.broadcasted_iota(jnp.int32, shape, 2)

    def below_y(v, h):
        w = jnp.where(sub3 == 0, 0.0 if h is None else h, roll(v, 1, 1))
        return roll(jnp.where(lane3 >= 96, w, v), 32, 2)

    def above_y(v, h):
        w = jnp.where(sub3 == 7, 0.0 if h is None else h, roll(v, -1, 1))
        return roll(jnp.where(lane3 < 32, w, v), -32, 2)

    def below_z(v, g):
        return jnp.where(lane3 % TILE == 0, roll(v, -31, 2), roll(v, 1, 2)) * g

    def above_z(v, g):
        return jnp.where(lane3 % TILE == TILE - 1, roll(v, 31, 2), roll(v, -1, 2)) * g

    def planes(x, n):
        return pl.ds(OFF + x, n)

    def velocity_planes(x, n, v_in, p_in, halo, v_out):
        here, under, over = planes(x, n), planes(x - 1, n), planes(x + 1, n)
        g_under, g_over, g_lo, g_hi = gate_x[here], gate_x[over], gate_lo[here], gate_hi[here]
        scale = RATE * ext[4, here]
        p = p_in[here]
        p_below = (p_in[under] * g_under, below_y(p, None if halo is None else halo[3, here]), below_z(p, g_lo))
        for d in range(3):
            v, h = v_in[d, here], None if halo is None else halo[d, here]
            total = (v_in[d, under] * g_under + v_in[d, over] * g_over) + (below_y(v, h) + above_y(v, h))
            total = total + (below_z(v, g_lo) + above_z(v, g_hi)) - 6.0 * v
            v_out[d, here] = v + scale * (force_ref[d] + total - (p - p_below[d]))

    def divergence_planes(x, n, v_in, halo_y):
        here, over = planes(x, n), planes(x + 1, n)
        vx, vy, vz = v_in[0, here], v_in[1, here], v_in[2, here]
        total = (v_in[0, over] * gate_x[over] - vx) + (above_y(vy, None if halo_y is None else halo_y[here]) - vy) + (above_z(vz, gate_hi[here]) - vz)
        return ext[4, here] * total

    step, shape3 = 5, (5, 8, 128)
    sub3, lane3 = iotas(shape3)
    for x in range(1, 31, step):
        velocity_planes(x, step, ext, ext.at[3], None, vel1)
        if x == 1:
            hear(0)
            tell(1, 2)
    for x, step in ((1, 5), (6, 5), (11, 5), (16, 5), (21, 5), (26, 4)):
        sub3, lane3 = iotas((step, 8, 128))
        pres1[planes(x, step)] = ext[3, planes(x, step)] + PRESSURE_RATE * divergence_planes(x, step, vel1, None)
    step = 4
    sub3, lane3 = iotas((step, 8, 128))
    for x in range(2, 30, step):
        velocity_planes(x, step, vel1, pres1, None, vel2)

    for copy in faces:
        copy.wait()

    row_lo, row_hi = ext[5, OFF - 1], ext[5, OFF + TILE]

    def spread_lo(tile):
        return jnp.where(lane < 64, tile, roll(tile, 64, 1))

    def spread_hi(tile):
        half = jnp.where(lane >= 96, tile, roll(tile, 96, 1))
        return jnp.where(lane >= 64, half, roll(half, 64, 1))

    corners = [recv_corner[k] for k in range(4)]
    col_lo, col_hi = spread_lo(recv_lo[2, 0:8]), spread_hi(recv_hi[1, 0:8])
    z_lo_outer = [(flag(corners[k], 6), flag(col, 4), flag(corners[k + 1], 6)) for k, col in ((0, col_lo), (2, col_hi))]
    z_hi_outer = [(flag(corners[k], 7), flag(col, 5), flag(corners[k + 1], 7)) for k, col in ((0, col_lo), (2, col_hi))]
    mid = [row_lo, own, row_hi]
    for k, x, n in ((0, OFF - 2, 2), (2, OFF + TILE, 3)):
        gate_lo[pl.ds(x, n)] = jnp.broadcast_to(jnp.where(depth == 0, flag(mid[k], 4), one)[None], (n, 8, 128))
        gate_hi[pl.ds(x, n)] = jnp.broadcast_to(jnp.where(depth == TILE - 1, flag(mid[k], 5), one)[None], (n, 8, 128))

    def by_region(tiles):
        return jnp.concatenate([tiles[0]] + [tiles[1]] * 4 + [tiles[2]], axis=0)

    def strip_gates(side, col, is_own, crossing, d):
        z_lo, z_hi, cross = [], [], []
        for k in range(3):
            z_lo.append(jnp.where(depth == 0, jnp.where(is_own, flag(mid[k], 4), z_lo_outer[side][k]), one))
            z_hi.append(jnp.where(depth == TILE - 1, jnp.where(is_own, flag(mid[k], 5), z_hi_outer[side][k]), one))
            cross.append(jnp.where(crossing, flag(mid[k], d), one))
        x_lo = jnp.where(sub == 0, jnp.where(is_own, flag(own, 0), flag(col, 0)), one)
        x_hi = jnp.where(sub == 0, jnp.where(is_own, flag(own, 1), flag(col, 1)), one)
        x_gate = jnp.concatenate([one, x_lo, one, one, one, x_hi], axis=0)
        return x_gate, by_region(cross), by_region(z_lo), by_region(z_hi)

    lo_gates = strip_gates(0, col_lo, lane >= 64, lane // TILE == 2, 2)
    hi_gates = strip_gates(1, col_hi, lane < 32, lane // TILE == 1, 3)
    cross_lo = by_region([flag(tile, 2) for tile in mid])
    cross_hi = by_region([flag(tile, 3) for tile in mid])

    def strip(received, tiles, g):
        return jnp.concatenate([roll(tiles[0], 6 - 2 * g, 0), received[g], roll(tiles[1], -2 * g, 0)], axis=0)

    raw = [strip(recv_lo, corners[:2], g) for g in range(3)]
    outer = [roll(raw[0], 64, 1), raw[0], roll(raw[1], 64, 1), raw[1], roll(raw[2], 64, 1)]
    lo = [jnp.where(lane_long < 64, outer[f], roll(ext[f, :, 0, :], 64, 1)) for f in range(5)]
    raw = [strip(recv_hi, corners[2:], g) for g in range(3)]
    outer = [roll(raw[0], 32, 1), roll(raw[1], 32, 1), roll(raw[0], 96, 1), roll(raw[2], 32, 1), roll(raw[2], 96, 1)]
    hi = [jnp.where(lane_long < 32, roll(ext[f, :, 7, :], 32, 1), outer[f]) for f in range(5)]

    depth_long = lane_long % TILE

    def strip_below(v, gates):
        x_gate, y_gate, z_lo, _ = gates
        return (
            roll(v, 1, 0) * x_gate,
            roll(v, 32, 1) * y_gate,
            jnp.where(depth_long == 0, roll(v, -31, 1), roll(v, 1, 1)) * z_lo,
        )

    def strip_above(v, gates):
        x_gate, y_gate, _, z_hi = gates
        return (
            roll(v * x_gate, -1, 0),
            roll(v * y_gate, -32, 1),
            jnp.where(depth_long == TILE - 1, roll(v, 31, 1), roll(v, -1, 1)) * z_hi,
        )

    def strip_velocity(v, p, m, gates, wanted):
        under = strip_below(p, gates)
        result = []
        for d in wanted:
            b, a = strip_below(v[d], gates), strip_above(v[d], gates)
            laplace = (b[0] + a[0]) + (b[1] + a[1]) + (b[2] + a[2]) - 6.0 * v[d]
            result.append(v[d] + RATE * m * (force_ref[d] + laplace - (p - under[d])))
        return result

    def strip_pressure(v, p, m, gates):
        total = zero_strip
        for d in range(3):
            total = total + (strip_above(v[d], gates)[d] - v[d])
        return p + PRESSURE_RATE * (m * total)

    zero_strip = jnp.zeros((PLANES, 128), f32)

    def put_hi(dst, v):
        dst[:, 7, :] = roll(v, 96, 1) * cross_hi

    lo1 = strip_velocity(lo[:3], lo[3], lo[4], lo_gates, (0, 1, 2))
    hi1 = strip_velocity(hi[:3], hi[3], hi[4], hi_gates, (0, 1, 2))
    lo_p1 = strip_pressure(lo1, lo[3], lo[4], lo_gates)
    hi_p1 = strip_pressure(hi1, hi[3], hi[4], hi_gates)

    for x, step in ((-1, 2), (31, 3)):
        sub3, lane3 = iotas((step, 8, 128))
        velocity_planes(x, step, ext, ext.at[3], None, vel1)
    scale_lo, scale_hi = RATE * ext[4, :, 0, :], RATE * ext[4, :, 7, :]
    for d in range(3):
        face = lo[d] + lo[3] if d == 1 else lo[d]
        vel1[d, :, 0, :] = vel1[d, :, 0, :] + jnp.where(lane_long < 32, scale_lo * (roll(face, 96, 1) * cross_lo), 0.0)
        vel1[d, :, 7, :] = vel1[d, :, 7, :] + jnp.where(lane_long >= 96, scale_hi * (roll(hi[d], 64, 1) * cross_hi), 0.0)

    hear(1)
    tell(2, 4)
    tell(3, 1)

    for x, step in ((-1, 2), (30, 3)):
        sub3, lane3 = iotas((step, 8, 128))
        pres1[planes(x, step)] = ext[3, planes(x, step)] + PRESSURE_RATE * divergence_planes(x, step, vel1, None)

    x_own = jnp.concatenate([one, jnp.where(sub == 0, flag(own, 0), one), one, one, one, jnp.where(sub == 0, flag(own, 1), one)], axis=0)
    z_lo_own = by_region([jnp.where(depth == 0, flag(tile, 4), one) for tile in mid])
    z_hi_own = by_region([jnp.where(depth == TILE - 1, flag(tile, 5), one) for tile in mid])

    def edge_below(v, under_y):
        return (
            roll(v, 1, 0) * x_own,
            jnp.where(lane_long < 32, under_y, roll(v, 32, 1)),
            jnp.where(depth_long == 0, roll(v, -31, 1), roll(v, 1, 1)) * z_lo_own,
        )

    def edge_above(v, over_y):
        return (
            roll(v * x_own, -1, 0),
            jnp.where(lane_long >= 96, over_y, roll(v, -32, 1)),
            jnp.where(depth_long == TILE - 1, roll(v, 31, 1), roll(v, -1, 1)) * z_hi_own,
        )

    def over_edge(ref, strip_values, s):
        return roll(ref[:, 1, :], 96, 1) if s == 0 else roll(strip_values, 64, 1) * cross_hi

    def under_edge(ref, strip_values, s):
        return roll(strip_values, 96, 1) * cross_lo if s == 0 else roll(ref[:, 6, :], 32, 1)

    for s in (0, 7):
        total = zero_strip
        for d in range(3):
            v = vel1[d, :, s, :]
            total = total + (edge_above(v, over_edge(vel1.at[d], hi1[d], s))[d] - v)
        pres1[:, s, :] = ext[3, :, s, :] + PRESSURE_RATE * (ext[4, :, s, :] * total)

    hi1_full = [jnp.where(lane_long < 32, roll(vel1[d, :, 7, :], 32, 1), hi1[d]) for d in range(3)]
    hi_p1 = jnp.where(lane_long < 32, roll(pres1[:, 7, :], 32, 1), hi_p1)
    put_hi(halo2, strip_velocity(hi1_full, hi_p1, hi[4], hi_gates, (1,))[0])

    for x, step in ((0, 2), (30, 3)):
        sub3, lane3 = iotas((step, 8, 128))
        velocity_planes(x, step, vel1, pres1, None, vel2)
    for s in (0, 7):
        p, scale = pres1[:, s, :], RATE * ext[4, :, s, :]
        p_below = edge_below(p, under_edge(pres1, lo_p1, s))
        for d in range(3):
            v = vel1[d, :, s, :]
            b = edge_below(v, under_edge(vel1.at[d], lo1[d], s))
            a = edge_above(v, over_edge(vel1.at[d], hi1[d], s))
            laplace = (b[0] + a[0]) + (b[1] + a[1]) + (b[2] + a[2]) - 6.0 * v
            vel2[d, :, s, :] = v + scale * (force_ref[d] + laplace - (p - p_below[d]))

    step = 8
    sub3, lane3 = iotas((step, 8, 128))
    message = zero
    for x in range(0, TILE, step):
        div = divergence_planes(x, step, vel2, halo2)
        pres2[pl.ds(x, step)] = pres1[planes(x, step)] + PRESSURE_RATE * div
        part = jnp.sum(div, axis=0)
        for shift in (1, 2, 4):
            part = part + jnp.where((lane // shift) % 2 == 0, roll(part, -shift, 1), roll(part, shift, 1))
        part = part + roll(part, 32, 1)
        part = part + roll(part, 64, 1)
        part = part + jnp.where(sub % 2 == 0, roll(part, -1, 0), roll(part, 1, 0))
        message = jnp.where(jnp.logical_and(2 * (lane // 32) + (lane % 8) // 4 == x // 8, sub == 2 * (lane % 4)), part, message)
    table[0, z_count // 2] = jnp.sum(message, axis=0, keepdims=True)[:, :64] * (1.0 / 64.0)

    middle = z_count // 2

    def straight_copy(dy, at):
        return pltpu.make_async_remote_copy(
            src_ref=table.at[0, pl.ds(middle, 1)], dst_ref=straight.at[pl.ds(c, 1)], send_sem=dsend_sem.at[dy * MID + at], recv_sem=drecv_sem.at[0],
            device_id=(r, lax.rem(y + dy, y_count) * z_count + at), device_id_type=MESH)

    def straight_goes(dy, at):
        goes = z != at if dy == 0 else None
        if at == 0:
            awake = jnp.logical_or(r > 0, lax.rem(y + dy, y_count) > 0)
            goes = awake if goes is None else jnp.logical_and(goes, awake)
        return goes

    def for_each_straight(act):
        for at in range(MID):
            for dy in (2, 1, y_count - 1, 0) if at < DIRECT else (0,):
                goes = straight_goes(dy, at)
                if goes is None:
                    act(straight_copy(dy, at))
                else:
                    pl.when(goes)(functools.partial(act, straight_copy(dy, at)))

    for_each_straight(lambda copy: copy.start())

    hear(3)
    near = []
    for k in range(1, NEAR + 1):
        for sign in (1, -1):
            index = len(near)
            near.append(pltpu.make_async_remote_copy(
                src_ref=table.at[0, middle], dst_ref=table.at[0, middle - sign * k], send_sem=gsend_sem.at[index], recv_sem=grecv_sem.at[index],
                device_id=along(0, sign * k), device_id_type=MESH))
    for copy in reversed(near):
        copy.start()

    stores = []
    for s in range(8):
        lanes = pl.ds(128 * s, 128)
        stores.append(pltpu.make_async_copy(vel2.at[:, pl.ds(OFF, TILE), s], fields_out.at[pl.ds(0, 3), :, lanes], store_sem.at[s]))
        stores.append(pltpu.make_async_copy(pres2.at[:, s], fields_out.at[3, :, lanes], store_sem.at[8 + s]))
    for copy in stores:
        copy.start()

    hear(2)
    tell(4, 3)
    hear(5)

    for copy in near:
        copy.wait()
    hear(4)
    width = 2 * NEAR + 1
    block, below_block, above_block = pl.ds(middle - NEAR, width), pl.ds(0, width), pl.ds(2 * FAR, width)
    far = []
    for k, (sign, landed) in enumerate(((1, below_block), (-1, above_block))):
        far.append(pltpu.make_async_remote_copy(
            src_ref=table.at[0, block], dst_ref=table.at[0, landed], send_sem=gsend_sem.at[len(near) + k], recv_sem=grecv_sem.at[len(near) + k],
            device_id=along(0, sign * FAR), device_id_type=MESH))
    wanted = [lax.rem(z + sign * FAR + z_count, z_count) >= MID for sign in (1, -1)]
    for copy, needed in zip(far, wanted, strict=True):
        pl.when(needed)(copy.start)

    def y_copies(parts, first):
        result = []
        for j in range(1, y_count):
            for part in parts:
                index = first + len(result)
                result.append(pltpu.make_async_remote_copy(
                    src_ref=table.at[0, part], dst_ref=table.at[y_count - j, part], send_sem=gsend_sem.at[index], recv_sem=grecv_sem.at[index],
                    device_id=along(j, 0), device_id_type=MESH))
        return result

    across = y_copies([block], len(near) + 2)
    across_far = y_copies([below_block, above_block], len(near) + 2 + len(across))

    @pl.when(z >= MID)
    def _():
        for copy in across:
            copy.start()
        for copy in far:
            copy.wait_recv()
        for copy in across_far:
            copy.start()

    spot = lax.broadcasted_iota(jnp.int32, (64, 512), 1)
    entry = spot // 128 % 2 * 32 + spot % 4 * 8 + spot // 64 % 2 * 4 + spot // 8 % 4
    pick = jnp.where(lax.broadcasted_iota(jnp.int32, (64, 512), 0) == entry, 1.0, 0.0).astype(f32)
    spot = lax.broadcasted_iota(jnp.int32, (8, 512), 1)
    octant = spot // 256 * 4 + (spot // 32) % 2 * 2 + (spot // 4) % 2
    holds = lax.broadcasted_iota(jnp.int32, (8, 512), 0) == octant

    for copy, needed in zip(far, wanted, strict=True):
        pl.when(needed)(copy.wait_send)
    for_each_straight(lambda copy: copy.wait_send())

    sources = [source_ref[0, o] for o in range(8)]
    kept = [jnp.maximum(source, 0) for source in sources]

    def keep(o, taken):
        row_buf[pl.ds(o, 1), :] = jnp.where(sources[o] >= 0, taken, jnp.zeros_like(taken))

    def arrive(count):
        straight[pl.ds(c, 1)] = table[0, pl.ds(middle, 1)]
        arrived = straight.at[pl.ds(0, count)]
        pltpu.make_async_copy(arrived, arrived, drecv_sem.at[0]).wait()

    handed = pltpu.make_async_remote_copy(
        src_ref=straight, dst_ref=straight, send_sem=dsend_sem.at[y_count * MID], recv_sem=drecv_sem.at[1], device_id=(r, 0 * c), device_id_type=MESH)
    hands_on = jnp.logical_and(r == 0, c == cols - z_count + MID - 1)

    @pl.when(jnp.logical_and(is_direct, jnp.logical_not(is_late)))
    def _():
        arrive(cols - 1)

    @pl.when(is_mid)
    def _():
        arrive(z_count - 1)
        ring = straight.at[pl.ds(y * z_count, z_count)]
        shares = [
            pltpu.make_async_remote_copy(
                src_ref=ring, dst_ref=ring, send_sem=dsend_sem.at[y_count * MID + j], recv_sem=drecv_sem.at[1 + j], device_id=along(j, 0), device_id_type=MESH)
            for j in range(1, y_count)
        ]
        for copy in shares:
            copy.start()
        for copy in shares:
            copy.wait()

    pl.when(hands_on)(handed.start)
    pl.when(is_late)(handed.wait_recv)

    @pl.when(z < MID)
    def _():
        for o in range(8):
            keep(o, straight[kept[o]])

    @pl.when(z >= MID)
    def _():
        for copy in across + across_far:
            copy.wait()
        for o in range(8):
            dy = lax.rem(kept[o] // z_count - y + y_count, y_count)
            dz = lax.rem(lax.rem(kept[o], z_count) - z + z_count + middle, z_count)
            keep(o, table[dy, dz])

    spread = jnp.dot(row_buf[...], pick, preferred_element_type=f32, precision=lax.Precision.HIGHEST)
    coarse_out[...] = jnp.sum(jnp.where(holds, spread, 0.0), axis=0, keepdims=True)

    for copy in stores:
        copy.wait()
    pl.when(hands_on)(handed.wait_send)


def on_device(rows, fields, fluid_mask, body_force, neighbours, sources):
    y_count, z_count = 4, 32
    f32 = jnp.float32
    volume = lambda n: pltpu.VMEM((n, PLANES, 8, 128), f32)
    planes = lambda: pltpu.VMEM((PLANES, 8, 128), f32)
    any_space = pl.BlockSpec(memory_space=pl.ANY)
    hbm = pl.BlockSpec(memory_space=pltpu.HBM)
    new_fields, coarse = pl.pallas_call(
        functools.partial(kernel, rows, y_count, z_count),
        out_shape=(
            jax.ShapeDtypeStruct((4, TILE, TILE * TILE), f32),
            jax.ShapeDtypeStruct((1, 512), f32),
        ),
        in_specs=[hbm] * 5,
        out_specs=(any_space, pl.BlockSpec(memory_space=pltpu.VMEM)),
        scratch_shapes=[
            pltpu.SMEM((1, 6), jnp.int32),
            pltpu.SMEM((1, 8), jnp.int32),
            pltpu.SMEM((3,), f32),
            volume(6),
            pltpu.VMEM((TILE, 8, 128), jnp.int32),
            volume(3),
            planes(),
            volume(3),
            pltpu.VMEM((TILE, 8, 128), f32),
            planes(),
            planes(),
            planes(),
            planes(),
            pltpu.VMEM((3, TILE, 128), f32),
            pltpu.VMEM((3, TILE, 128), f32),
            pltpu.VMEM((3, TILE, 128), f32),
            pltpu.VMEM((3, TILE, 128), f32),
            pltpu.VMEM((4, 8, 128), f32),
            pltpu.VMEM((4, 8, 128), f32),
            pltpu.VMEM((y_count, SLOTS, 1, 64), f32),
            pltpu.VMEM((y_count * z_count, 1, 64), f32),
            pltpu.VMEM((8, 64), f32),
            pltpu.SemaphoreType.DMA((19,)),
            pltpu.SemaphoreType.DMA((16,)),
            pltpu.SemaphoreType.DMA((8,)),
            pltpu.SemaphoreType.DMA((8,)),
            pltpu.SemaphoreType.DMA((GATHER_COPIES,)),
            pltpu.SemaphoreType.DMA((GATHER_COPIES,)),
            pltpu.SemaphoreType.DMA((y_count * MID + y_count,)),
            pltpu.SemaphoreType.DMA((1 + y_count,)),
            pltpu.SemaphoreType.REGULAR((6,)),
        ],
        compiler_params=pltpu.CompilerParams(
            collective_id=0, has_side_effects=True, vmem_limit_bytes=32 * 1024 * 1024
        ),
    )(
        *(
            pltpu.with_memory_space_constraint(array, pltpu.HBM)
            for array in (
                neighbours,
                sources,
                body_force,
                fields.reshape(4, TILE, TILE * TILE),
                fluid_mask.reshape(TILE, TILE * TILE),
            )
        )
    )
    return new_fields[None], coarse


def solution(mesh):
    return jax.shard_map(
        functools.partial(on_device, mesh.shape["row"]),
        mesh=mesh,
        in_specs=(
            P(("row", "col"), None, None, None),
            P(("row", "col"), None, None),
            P(),
            P(("row", "col"), None),
            P(("row", "col"), None),
        ),
        out_specs=(P(("row", "col"), None, None, None), P(("row", "col"), None)),
        check_vma=False,
    )
```
